32 devices in a mesh: row: 4 (over x, core), col: 8 (over z, y).
Axes of the slice: x: 2, y: 2, z: 4, core: 2. Of those that a mesh axis runs over, the one named last changes fastest.
Arguments:
- density: bfloat16 [2048, 2048], P('row', 'col'), may hold values from -2 to 2
- core_ham: float32 [2048, 2048], P('row', 'col'), may hold values from -6 to 6
- block_mask: int32 [32, 32], P('row', 'col'), may hold values 0 or 1
- send_blocks: int32 [32, 32, 8], P(('row', 'col')), may hold values from -1 to 31, as said below
- task_atoms: int32 [2, 32, 32, 8], P(None, ('row', 'col')), may hold values from 0 to 15
- basis: bfloat16 [32, 1024, 2048], P(('row', 'col')), may hold values from -0.375 to 0.375
- v_loc: float32 [32, 2048], P(('row', 'col')), may hold values from -6 to 6
Outputs:
- ks_matrix: float32 [2048, 2048], P('row', 'col')
- sign_step: float32 [2048, 2048], P('row', 'col')
The draws below stay inside these ranges and needn't reach their ends.
Inputs may be any that keep to these rules, and one draw needn't show every extreme that they name: In each list send_blocks[o, e] the live entries come first and the rest are -1; every list has one live entry or more, and in every draw some sub-slab receives all 8 slots live from every owner.
All inputs are finite; a program needn't handle non-finite values. No bound on the sum of `block_mask` on one device may be relied on, other than what follows from the above.
Results may differ from the reference program's by a relative error of at most 0.0048.
Values may be sent and summed in bfloat16 or wider, within the bound.
A program may use at most 64 MiB of HBM per device.

```python
import math
import jax
import jax.numpy as jnp
from jax import lax

BLK = 64
BC = 4
CELLS = 2048
ATOMS = 16
CAP = 8
NBLK = 32
BR = 8
NMAT = 2048
N_ROW = 4
N_COL = 8
DEVICES = 32


def draw_send_blocks(key, part):
    key_count = jax.random.fold_in(key, 11)
    key_full = jax.random.fold_in(key, 12)
    key_block = jax.random.fold_in(key, 13)
    counts = jax.random.randint(key_count, (DEVICES, DEVICES), 1, CAP + 1)
    full_dest = jax.random.randint(key_full, (), 0, DEVICES)
    counts = jnp.where(jnp.arange(DEVICES)[None, :] == full_dest, CAP, counts)
    numbers = jax.random.randint(key_block, (DEVICES, DEVICES, CAP), 0, BR * BC)
    slots = jnp.arange(CAP)[None, None, :]
    return jnp.where(slots < counts[:, :, None], numbers, -1).astype(jnp.int32)


def touch_ends(result, rng, least, top_value):
    longest = result.shape.index(max(result.shape))
    spots = []
    for shift in (0, 1):
        where = [jax.random.randint(jax.random.fold_in(rng, axis), (), 0, length) for axis, length in enumerate(result.shape)]
        where[longest] = (where[longest] + shift) % result.shape[longest]
        spots.append(tuple(where))
    return result.at[spots[0]].set(least).at[spots[1]].set(top_value)


def shard_levels(stream_key, extent, cuts, least, largest):
    factor_of = 1.0
    for dim, blocks in cuts:
        heights = jax.random.uniform(jax.random.fold_in(jax.random.fold_in(stream_key, 6), dim), (blocks,), jnp.float32, least / len(cuts), largest / len(cuts))
        factor_of = factor_of * jnp.repeat(jnp.exp(heights), extent[dim] // blocks).reshape((-1,) + (1,) * (len(extent) - 1 - dim))
    return factor_of


def scatter_about(rng, extent, deviation, bound, cuts=(), kind=jnp.bfloat16):
    gain = shard_levels(rng, extent, cuts, -0.22, 0.18) if cuts else 1.0
    values = jax.random.normal(rng, extent, jnp.float32) * deviation * gain
    return jnp.minimum(jnp.maximum(values, -bound), bound).astype(kind)


def setup_inputs(seed: int = 0) -> dict:
    key_list = jax.random.split(jax.random.key(seed), 8)
    return {
        "density": scatter_about(key_list[0], (NMAT, NMAT), 0.125, 2.0, ((0, 4), (1, 8))),
        "core_ham": scatter_about(key_list[1], (NMAT, NMAT), 1.0, 6.0, ((0, 4), (1, 8)), jnp.float32),
        "block_mask": touch_ends((jax.random.randint(key_list[2], (NBLK, NBLK), 0, 3) < 1).astype(jnp.int32), jax.random.fold_in(key_list[2], 1), 0, 1),
        "send_blocks": draw_send_blocks(jax.random.fold_in(key_list[7], 71), 0),
        "task_atoms": touch_ends(jax.random.randint(key_list[4], (2, DEVICES, DEVICES, CAP), 0, ATOMS), jax.random.fold_in(key_list[4], 1), 0, ATOMS - 1).astype(jnp.int32),
        "basis": scatter_about(key_list[5], (DEVICES, ATOMS * BLK, CELLS), 256 ** -0.5, 0.375, ((0, 32),)),
        "v_loc": scatter_about(key_list[6], (DEVICES, CELLS), 1.0, 6.0, ((0, 32),), jnp.float32),
    }


def reference(density, core_ham, block_mask, send_blocks, task_atoms, basis, v_loc):
    local_count = BR * BC
    dens_blocks = density.reshape(N_ROW, BR, BLK, N_COL, BC, BLK).transpose(0, 3, 1, 4, 2, 5).reshape(DEVICES, local_count, BLK * BLK)
    owners = jnp.arange(DEVICES, dtype=jnp.int32)[:, None]
    pair_ids = jnp.arange(ATOMS * ATOMS, dtype=jnp.int32)

    def slab_step(ham_sum, slab):
        slots = lax.dynamic_index_in_dim(send_blocks, slab, 1, keepdims=False)
        live = slots >= 0
        safe = jnp.maximum(slots, 0).astype(jnp.int32)
        sent = dens_blocks[owners, safe] * live[:, :, None].astype(jnp.bfloat16)
        atoms = lax.dynamic_index_in_dim(task_atoms, slab, 1, keepdims=False)
        pair = (atoms[0] * ATOMS + atoms[1]).reshape(-1)
        onehot = (pair[:, None] == pair_ids[None, :]).astype(jnp.bfloat16)
        pair_sum = jnp.dot(onehot.T, sent.reshape(-1, BLK * BLK), preferred_element_type=jnp.float32)
        pair_mat = pair_sum.reshape(ATOMS, ATOMS, BLK, BLK).transpose(0, 2, 1, 3).reshape(ATOMS * BLK, ATOMS * BLK).astype(jnp.bfloat16)
        basis_vals = lax.dynamic_index_in_dim(basis, slab, 0, keepdims=False)
        mixed = jnp.dot(pair_mat, basis_vals, preferred_element_type=jnp.float32)
        rho = lax.optimization_barrier(jnp.sum(basis_vals.astype(jnp.float32) * mixed, axis=0))
        pot = lax.dynamic_index_in_dim(v_loc, slab, 0, keepdims=False) + 0.5 * rho / jnp.sqrt(1.0 + rho * rho)
        weighted = (basis_vals.astype(jnp.float32) * pot[None, :]).astype(jnp.bfloat16)
        k_all = jnp.dot(weighted, basis_vals.T, preferred_element_type=jnp.float32)
        k_pairs = k_all.reshape(ATOMS, BLK, ATOMS, BLK).transpose(0, 2, 1, 3).reshape(ATOMS * ATOMS, BLK * BLK)
        k_slot = k_pairs[pair].astype(jnp.bfloat16).reshape(DEVICES, CAP, BLK * BLK)
        added = jnp.where(live[:, :, None], k_slot.astype(jnp.float32), jnp.zeros((), jnp.float32))
        ham_sum = ham_sum.at[owners, safe].add(added)
        return (ham_sum, None)
    start = jnp.zeros((DEVICES, local_count, BLK * BLK), jnp.float32)
    ham_sum, _ = lax.scan(slab_step, start, jnp.arange(DEVICES, dtype=jnp.int32))
    ham_full = ham_sum.reshape(N_ROW, N_COL, BR, BC, BLK, BLK).transpose(0, 2, 4, 1, 3, 5).reshape(NMAT, NMAT)
    ks_matrix = core_ham + ham_full
    mask = jnp.broadcast_to(block_mask.astype(jnp.float32)[:, None, :, None], (NBLK, BLK, NBLK, BLK)).reshape(NMAT, NMAT)
    scale = 1.0 / math.sqrt(16.0 * NBLK)
    x0 = (mask * ks_matrix * scale).astype(jnp.bfloat16)
    x2 = (mask * jnp.dot(x0, x0, preferred_element_type=jnp.float32)).astype(jnp.bfloat16)
    x3 = mask * jnp.dot(x0, x2, preferred_element_type=jnp.float32)
    sign_step = (1.5 * x0.astype(jnp.float32) - 0.5 * x3) / scale
    return (ks_matrix, sign_step)
```

```python
import functools
import math

import jax
import jax.numpy as jnp
from jax import lax
from jax.experimental import pallas as pl
from jax.experimental.pallas import tpu as pltpu
from jax.sharding import PartitionSpec as P

ATOMS = 16
EDGE = 64
HALF = EDGE // 2
LANES = 2 * EDGE
CORES = 2
MESH = pl.DeviceIdType.MESH
VMEM_LIMIT = 56 * 1024 * 1024


def low_lanes():
    return lax.broadcasted_iota(jnp.int32, (HALF, LANES), 1) < EDGE


def join_pair(first, second):
    low = low_lanes()
    top = jnp.where(low, first, pltpu.roll(second, EDGE, 1))
    bottom = jnp.where(low, pltpu.roll(first, EDGE, 1), second)
    return top, bottom


def split_pair(top, bottom):
    return join_pair(top, bottom)


def pick_kernel(index_ref, density_ref, out_ref, packed):
    rows, cols = density_ref.shape
    across = cols // EDGE
    count = (rows // EDGE) * across
    packed[count] = jnp.zeros((HALF, LANES), packed.dtype)
    for i in range(rows // EDGE):
        for j in range(0, across, 2):
            lanes = slice(j * EDGE, (j + 2) * EDGE)
            top = density_ref[i * EDGE : i * EDGE + HALF, lanes].astype(jnp.float32)
            bottom = density_ref[i * EDGE + HALF : (i + 1) * EDGE, lanes].astype(jnp.float32)
            first, second = split_pair(top, bottom)
            packed[i * across + j] = first.astype(packed.dtype)
            packed[i * across + j + 1] = second.astype(packed.dtype)

    def copy_slot(slot, carry):
        out_ref[slot] = packed[index_ref[slot]]
        return carry

    lax.fori_loop(0, out_ref.shape[0], copy_slot, 0, unroll=8)


def pick_blocks(index, density):
    count = (density.shape[0] // EDGE) * (density.shape[1] // EDGE)
    return pl.pallas_call(
        pick_kernel,
        out_shape=jax.ShapeDtypeStruct((index.shape[0], HALF, LANES), jnp.bfloat16),
        in_specs=[pl.BlockSpec(memory_space=pltpu.SMEM), pl.BlockSpec(memory_space=pltpu.VMEM)],
        out_specs=pl.BlockSpec(memory_space=pltpu.VMEM),
        scratch_shapes=[pltpu.VMEM((count + 1, HALF, LANES), jnp.bfloat16)],
        compiler_params=pltpu.CompilerParams(vmem_limit_bytes=VMEM_LIMIT),
        name="pick",
    )(index, density)


def grid_kernel(chunk, pair_ref, recv_ref, basis_ref, vloc_ref, out_ref, sums, pair_mat, k_all):
    cells = basis_ref.shape[1]
    sums[...] = jnp.zeros_like(sums)
    k_all[...] = jnp.zeros_like(k_all)

    def add_slot(slot, carry):
        at = pair_ref[slot]
        sums[at] = sums[at] + recv_ref[slot].astype(jnp.float32)
        return carry

    lax.fori_loop(0, recv_ref.shape[0], add_slot, 0, unroll=8)

    def assemble(a, carry):
        row = pl.multiple_of(a * EDGE, EDGE)
        for b in range(0, ATOMS, 2):
            top, bottom = join_pair(sums[a * ATOMS + b], sums[a * ATOMS + b + 1])
            lanes = slice(b * EDGE, (b + 2) * EDGE)
            pair_mat[pl.ds(row, HALF), lanes] = top.astype(jnp.bfloat16)
            pair_mat[pl.ds(row + HALF, HALF), lanes] = bottom.astype(jnp.bfloat16)
        return carry

    lax.fori_loop(0, ATOMS, assemble, 0)

    def integrate(step, carry):
        at = pl.ds(pl.multiple_of(step * chunk, chunk), chunk)
        vals = basis_ref[:, at]
        mixed = jnp.dot(pair_mat[...], vals, preferred_element_type=jnp.float32)
        wide = vals.astype(jnp.float32)
        rho = jnp.sum(wide * mixed, axis=0, keepdims=True)
        pot = vloc_ref[:, at] + 0.5 * rho / jnp.sqrt(1.0 + rho * rho)
        weighted = (wide * pot).astype(jnp.bfloat16)
        k_all[...] += lax.dot_general(
            weighted, vals, (((1,), (1,)), ((), ())), preferred_element_type=jnp.float32
        )
        return carry

    lax.fori_loop(0, cells // chunk, integrate, 0)

    def split(a, carry):
        row = pl.multiple_of(a * EDGE, EDGE)
        for b in range(0, ATOMS, 2):
            lanes = slice(b * EDGE, (b + 2) * EDGE)
            first, second = split_pair(k_all[pl.ds(row, HALF), lanes], k_all[pl.ds(row + HALF, HALF), lanes])
            sums[a * ATOMS + b] = first
            sums[a * ATOMS + b + 1] = second
        return carry

    lax.fori_loop(0, ATOMS, split, 0)

    def give_slot(slot, carry):
        out_ref[slot] = sums[pair_ref[slot]].astype(jnp.bfloat16)
        return carry

    lax.fori_loop(0, out_ref.shape[0], give_slot, 0, unroll=8)


def grid_step(pair, received, basis, v_loc):
    order = ATOMS * EDGE
    chunk = math.gcd(basis.shape[1], 512)
    return pl.pallas_call(
        functools.partial(grid_kernel, chunk),
        out_shape=jax.ShapeDtypeStruct(received.shape, jnp.bfloat16),
        in_specs=[pl.BlockSpec(memory_space=pltpu.SMEM)] + [pl.BlockSpec(memory_space=pltpu.VMEM)] * 3,
        out_specs=pl.BlockSpec(memory_space=pltpu.VMEM),
        scratch_shapes=[
            pltpu.VMEM((ATOMS * ATOMS, HALF, LANES), jnp.float32),
            pltpu.VMEM((order, order), jnp.bfloat16),
            pltpu.VMEM((order, order), jnp.float32),
        ],
        compiler_params=pltpu.CompilerParams(vmem_limit_bytes=VMEM_LIMIT),
        name="grid",
    )(pair, received, basis, v_loc)


def block_masks(mask_ref, i, j):
    low = lax.broadcasted_iota(jnp.int32, (EDGE, LANES), 1) < EDGE
    return jnp.where(low, mask_ref[i, j].astype(jnp.float32), mask_ref[i, j + 1].astype(jnp.float32))


def add_kernel(scale, index_ref, mask_ref, back_ref, core_ref, ks_ref, x0_ref, sums):
    rows, cols = core_ref.shape
    across = cols // EDGE
    sums[...] = jnp.zeros_like(sums)

    def add_slot(slot, carry):
        at = index_ref[slot]
        sums[at] = sums[at] + back_ref[slot].astype(jnp.float32)
        return carry

    lax.fori_loop(0, back_ref.shape[0], add_slot, 0, unroll=8)
    for i in range(rows // EDGE):
        for j in range(0, across, 2):
            lanes = slice(j * EDGE, (j + 2) * EDGE)
            high, mid, low = i * EDGE, i * EDGE + HALF, (i + 1) * EDGE
            top, bottom = join_pair(sums[i * across + j], sums[i * across + j + 1])
            ks_ref[high:mid, lanes] = core_ref[high:mid, lanes] + top
            ks_ref[mid:low, lanes] = core_ref[mid:low, lanes] + bottom
            kept = block_masks(mask_ref, i, j) * ks_ref[high:low, lanes] * scale
            x0_ref[high:low, lanes] = kept.astype(jnp.bfloat16)


def add_back(scale, index, block_mask, returned, core_ham):
    count = (core_ham.shape[0] // EDGE) * (core_ham.shape[1] // EDGE)
    return pl.pallas_call(
        functools.partial(add_kernel, scale),
        out_shape=(
            jax.ShapeDtypeStruct(core_ham.shape, jnp.float32),
            jax.ShapeDtypeStruct(core_ham.shape, jnp.bfloat16),
        ),
        in_specs=[pl.BlockSpec(memory_space=pltpu.SMEM)] * 2 + [pl.BlockSpec(memory_space=pltpu.VMEM)] * 2,
        out_specs=(pl.BlockSpec(memory_space=pltpu.VMEM),) * 2,
        scratch_shapes=[pltpu.VMEM((count + 1, HALF, LANES), jnp.float32)],
        compiler_params=pltpu.CompilerParams(vmem_limit_bytes=VMEM_LIMIT),
        name="add_back",
    )(index, block_mask, returned, core_ham)


class LineGather:
    def __init__(self, held, outer, inner, place, device_at, sems):
        self.held, self.outer, self.inner = held, outer, inner
        self.a, self.b = place // inner, place % inner
        self.device_at = device_at
        self.out_sem, self.in_sem, self.recv_sem = sems
        self.sent = []

    def neighbours(self):
        a, b = self.a, self.b
        return (
            (a > 0, a - 1, b),
            (a < self.outer - 1, a + 1, b),
            (b > 0, a, b - 1),
            (b < self.inner - 1, a, b + 1),
        )

    def send(self, cond, source, target, sem):
        def describe():
            return pltpu.make_async_remote_copy(
                src_ref=self.held.at[source],
                dst_ref=self.held.at[source],
                send_sem=sem,
                recv_sem=self.recv_sem.at[source],
                device_id=self.device_at(target),
                device_id_type=MESH,
            )

        @pl.when(cond)
        def _():
            describe().start()

        self.sent.append((cond, describe))

    def arrive(self, source):
        pltpu.make_async_copy(self.held.at[source], self.held.at[source], self.recv_sem.at[source]).wait()

    def along_inner(self, cond, outer_at, inner_from, step, sem):
        target = self.b + step
        fits = jnp.logical_and(target >= 0, target < self.inner)
        self.send(
            jnp.logical_and(cond, fits), outer_at * self.inner + inner_from, self.a * self.inner + target, sem
        )

    def steps(self):
        a, b, inner = self.a, self.b, self.inner
        for d in range(self.outer):
            for way, step in enumerate((1, -1)):
                if d == 0 and way == 1:
                    have = a >= 0
                    source = a
                else:
                    source = a - d * step
                    have = jnp.logical_and(source >= 0, source < self.outer)
                tile = source * inner + b
                if d > 0:

                    @pl.when(have)
                    def _():
                        self.arrive(tile)

                target = a + step
                fits = jnp.logical_and(target >= 0, target < self.outer)
                self.send(jnp.logical_and(have, fits), tile, target * inner + b, self.out_sem.at[d, way])
                if d > 0 or way == 0:
                    for side, hop in enumerate((1, -1)):
                        self.along_inner(have, source, b, hop, self.in_sem.at[d * 2 + way, side])
            yield
        used = 2 * self.outer
        for e in range(1, inner):
            for outer_at in range(self.outer):
                for way, step in enumerate((1, -1)):
                    origin = b - e * step
                    have = jnp.logical_and(origin >= 0, origin < inner)
                    tile = outer_at * inner + origin

                    @pl.when(have)
                    def _():
                        self.arrive(tile)

                    if e < inner - 1:
                        self.along_inner(have, outer_at, origin, step, self.in_sem.at[used, way])
                if e < inner - 1:
                    used += 1
            yield

    def drain(self):
        for cond, describe in self.sent:

            @pl.when(cond)
            def _():
                describe().wait_send()

    @staticmethod
    def semaphores(outer, inner):
        return [
            pltpu.SemaphoreType.DMA((outer, 2)),
            pltpu.SemaphoreType.DMA((2 * outer + max(inner - 2, 0) * outer, 2)),
            pltpu.SemaphoreType.DMA((outer * inner,)),
        ]


def greet(gathers):
    barrier = pltpu.get_barrier_semaphore()
    count = 0
    for gather in gathers:
        for cond, a, b in gather.neighbours():

            @pl.when(cond)
            def _():
                pl.semaphore_signal(
                    barrier, inc=1, device_id=gather.device_at(a * gather.inner + b), device_id_type=MESH
                )

            count = count + cond.astype(jnp.int32)
    pl.semaphore_wait(barrier, count)


def run_together(*gathers):
    going = [gather.steps() for gather in gathers]
    while going:
        going = [steps for steps in going if next(steps, "end") is None]


def panel_product(left, right, acc):
    height, width = right.shape[1], left.shape[2]
    acc[...] = jnp.zeros_like(acc)
    for j in range(left.shape[0]):
        start = j * width
        part = right[start // height, start % height : start % height + width, :]
        acc[...] += jnp.dot(left[j], part, preferred_element_type=jnp.float32)


def sign_kernel(scale, row_lines, col_lines, mask_ref, x0_ref, out_ref, left, right, second, mask, acc, *sems):
    row, col = lax.axis_index("row"), lax.axis_index("col")
    rows, cols = x0_ref.shape
    along_col = LineGather(left, *col_lines, col, lambda at: (row, at), sems[0:3])
    along_row = LineGather(right, *row_lines, row, lambda at: (at, col), sems[3:6])
    again = LineGather(second, *row_lines, row, lambda at: (at, col), sems[6:9])
    greet([along_col, along_row])
    left[col] = x0_ref[...]
    right[row] = x0_ref[...]
    run_together(along_col, along_row)
    for i in range(rows // EDGE):
        for j in range(0, cols // EDGE, 2):
            mask[i * EDGE : (i + 1) * EDGE, j * EDGE : (j + 2) * EDGE] = block_masks(mask_ref, i, j)
    panel_product(left, right, acc)
    second[row] = (mask[...] * acc[...]).astype(jnp.bfloat16)
    run_together(again)
    panel_product(left, second, acc)
    out_ref[...] = (1.5 * x0_ref[...].astype(jnp.float32) - 0.5 * (mask[...] * acc[...])) / scale
    for gather in (along_col, along_row, again):
        gather.drain()


def sign_step(scale, block_mask, x0):
    row_count, col_count = lax.axis_size("row"), lax.axis_size("col")
    row_lines = (row_count // CORES, CORES)
    outer = math.gcd(col_count, 4)
    col_lines = (outer, col_count // outer)
    rows, cols = x0.shape
    return pl.pallas_call(
        functools.partial(sign_kernel, scale, row_lines, col_lines),
        out_shape=jax.ShapeDtypeStruct(x0.shape, jnp.float32),
        in_specs=[pl.BlockSpec(memory_space=pltpu.SMEM), pl.BlockSpec(memory_space=pltpu.VMEM)],
        out_specs=pl.BlockSpec(memory_space=pltpu.VMEM),
        scratch_shapes=[
            pltpu.VMEM((col_count, rows, cols), jnp.bfloat16),
            pltpu.VMEM((row_count, rows, cols), jnp.bfloat16),
            pltpu.VMEM((row_count, rows, cols), jnp.bfloat16),
            pltpu.VMEM((rows, cols), jnp.float32),
            pltpu.VMEM((rows, cols), jnp.float32),
            *LineGather.semaphores(*col_lines),
            *LineGather.semaphores(*row_lines),
            *LineGather.semaphores(*row_lines),
        ],
        compiler_params=pltpu.CompilerParams(
            vmem_limit_bytes=VMEM_LIMIT, collective_id=0, has_side_effects=True
        ),
        name="sign",
    )(block_mask, x0)


def exchange(blocks, device_count):
    parts = blocks.reshape(device_count, blocks.shape[0] // device_count, HALF, LANES)
    return lax.all_to_all(parts, ("row", "col"), split_axis=0, concat_axis=0, tiled=True).reshape(blocks.shape)


def body(density, core_ham, block_mask, send_blocks, task_atoms, basis, v_loc):
    row_count = lax.axis_size("row")
    device_count = row_count * lax.axis_size("col")
    block_rows = density.shape[0] // EDGE
    local_count = block_rows * (density.shape[1] // EDGE)
    slots = send_blocks[0].reshape(-1)
    index = jnp.where(slots >= 0, slots, local_count)
    atoms = task_atoms[:, 0]
    pair = (atoms[0] * ATOMS + atoms[1]).reshape(-1)
    received = exchange(pick_blocks(index, density), device_count)
    k_slot = grid_step(pair, received, basis[0], v_loc)
    returned = exchange(k_slot, device_count)
    scale = 1.0 / math.sqrt(16.0 * block_rows * row_count)
    ks_matrix, x0 = add_back(scale, index, block_mask, returned, core_ham)
    return (ks_matrix, sign_step(scale, block_mask, x0))


def solution(mesh):
    placed = (
        P("row", "col"),
        P("row", "col"),
        P("row", "col"),
        P(("row", "col"), None, None),
        P(None, ("row", "col"), None, None),
        P(("row", "col"), None, None),
        P(("row", "col"), None),
    )
    return jax.shard_map(
        body,
        mesh=mesh,
        in_specs=placed,
        out_specs=(P("row", "col"), P("row", "col")),
        check_vma=False,
    )
```

```python
import functools
import math

import jax
import jax.numpy as jnp
from jax import lax
from jax.experimental import pallas as pl
from jax.experimental.pallas import tpu as pltpu
from jax.sharding import PartitionSpec as P

ATOMS = 16
EDGE = 64
HALF = EDGE // 2
LANES = 2 * EDGE
CORES = 2
MESH = pl.DeviceIdType.MESH
VMEM_LIMIT = 56 * 1024 * 1024


def low_lanes():
    return lax.broadcasted_iota(jnp.int32, (HALF, LANES), 1) < EDGE


def join_pair(first, second):
    low = low_lanes()
    top = jnp.where(low, first, pltpu.roll(second, EDGE, 1))
    bottom = jnp.where(low, pltpu.roll(first, EDGE, 1), second)
    return top, bottom


def split_pair(top, bottom):
    return join_pair(top, bottom)


class Plane:
    def __init__(self, outer, inner, row_count):
        self.outer, self.inner, self.count = outer, inner, row_count * inner
        self.row, col = lax.axis_index("row"), lax.axis_index("col")
        self.a, self.b = col // inner, col % inner
        self.place = self.row * inner + self.b

    def peer(self, offset):
        return lax.rem(self.place + 1 + offset, self.count)

    def device(self, place):
        return (place // self.inner, self.a * self.inner + place % self.inner)

    def owner(self, place, outer_at):
        return (place // self.inner) * (self.outer * self.inner) + outer_at * self.inner + place % self.inner

    def on_line(self, outer_at):
        return (self.row, outer_at * self.inner + self.b)

    def greet(self, line):
        barrier = pltpu.get_barrier_semaphore()

        def signal(offset, carry):
            pl.semaphore_signal(barrier, inc=1, device_id=self.device(self.peer(offset)), device_id_type=MESH)
            return carry

        lax.fori_loop(0, self.count - 1, signal, 0)
        greet([line], self.count - 1)


def send_kernel(
    outer, inner, row_count, index_ref, lists_ref, density_ref, out_ref, kept_ref,
    own, lists, lists_smem, stage, list_sem, recv_sem, send_sem, tile_send, tile_recv, *rest
):
    plane = Plane(outer, inner, row_count)
    a = plane.a
    rows, cols = density_ref.shape
    across = cols // EDGE
    count = (rows // EDGE) * across
    slots = stage.shape[2]
    entries = LineGather(lists.at.__getitem__, outer, 1, a, plane.on_line, rest[0:3])
    arrived = (rest[3 : 2 + outer], rest[2 + outer :])
    for tile in (own, *arrived[0], *arrived[1]):
        tile[count] = jnp.zeros((HALF, LANES), tile.dtype)
    plane.greet(entries)
    lists[a] = lists_ref[...]
    for i in range(rows // EDGE):
        for j in range(0, across, 2):
            lanes = slice(j * EDGE, (j + 2) * EDGE)
            top = density_ref[i * EDGE : i * EDGE + HALF, lanes].astype(jnp.float32)
            bottom = density_ref[i * EDGE + HALF : (i + 1) * EDGE, lanes].astype(jnp.float32)
            first, second = split_pair(top, bottom)
            own[i * across + j] = first.astype(own.dtype)
            own[i * across + j + 1] = second.astype(own.dtype)

    def passes(d, step):
        source, target = a - d * step, a + step
        return jnp.logical_and(
            jnp.logical_and(source >= 0, source < outer), jnp.logical_and(target >= 0, target < outer)
        )

    def pass_on(d, way, step):
        tile = arrived[way][d - 1] if d else own
        return pltpu.make_async_remote_copy(
            src_ref=tile.at[pl.ds(0, count)],
            dst_ref=arrived[way][d].at[pl.ds(0, count)],
            send_sem=tile_send.at[way, d],
            recv_sem=tile_recv.at[way, d],
            device_id=plane.on_line(a + step),
            device_id_type=MESH,
        )

    def serve(tile, source, number):
        def pick(offset, place):
            for slot in range(slots):
                stage[source, offset, slot] = tile[number(place * slots + slot)]

        def one(offset, carry):
            place = plane.peer(offset)
            pick(offset, place)
            pltpu.make_async_remote_copy(
                src_ref=stage.at[source, offset],
                dst_ref=out_ref.at[plane.owner(plane.place, source)],
                send_sem=send_sem,
                recv_sem=recv_sem,
                device_id=plane.device(place),
                device_id_type=MESH,
            ).start()
            return carry

        lax.fori_loop(0, plane.count - 1, one, 0)
        pick(plane.count - 1, plane.place)
        pltpu.make_async_copy(
            stage.at[source, plane.count - 1], out_ref.at[plane.owner(plane.place, source)], recv_sem
        ).start()

    entry_steps = entries.steps()
    for d in range(outer):
        next(entry_steps)
        if d:
            for way, step in enumerate((1, -1)):

                @pl.when(jnp.logical_and(a - d * step >= 0, a - d * step < outer))
                def _():
                    tile = arrived[way][d - 1].at[pl.ds(0, count)]
                    pltpu.make_async_copy(tile, tile, tile_recv.at[way, d - 1]).wait()

        if d < outer - 1:
            for way, step in enumerate((1, -1)):

                @pl.when(passes(d, step))
                def _():
                    pass_on(d, way, step).start()

        if d == 0:
            serve(own, a, lambda at: index_ref[a, at])
            continue
        for way, step in enumerate((1, -1)):
            source = a - d * step

            @pl.when(jnp.logical_and(source >= 0, source < outer))
            def _():
                copy = pltpu.make_async_copy(lists.at[source], lists_smem.at[source], list_sem)
                copy.start()
                copy.wait()
                serve(arrived[way][d - 1], source, lambda at: lists_smem[source, a, at])

    kept_ref[...] = jnp.zeros_like(kept_ref)
    for i in range(outer):
        kept_ref[i : i + 1, :] = lists[i, pl.ds(a, 1), :]
    for d in range(outer - 1):
        for way, step in enumerate((1, -1)):

            @pl.when(passes(d, step))
            def _():
                pass_on(d, way, step).wait_send()

    entries.drain()
    sent = stage.at[:, pl.ds(0, plane.count - 1)]
    pltpu.make_async_copy(sent, sent, send_sem).wait()
    pltpu.make_async_copy(out_ref, out_ref, recv_sem).wait()


def send_blocks_out(lines, slots, lists, density):
    outer, inner = lines
    row_count, col_count = lax.axis_size("row"), lax.axis_size("col")
    plane_count = row_count * inner
    count = (density.shape[0] // EDGE) * (density.shape[1] // EDGE)
    vmem = pl.BlockSpec(memory_space=pltpu.VMEM)
    return pl.pallas_call(
        functools.partial(send_kernel, outer, inner, row_count),
        out_shape=(
            jax.ShapeDtypeStruct((row_count * col_count, slots, HALF, LANES), jnp.bfloat16),
            jax.ShapeDtypeStruct(lists.shape, jnp.int32),
        ),
        in_specs=[pl.BlockSpec(memory_space=pltpu.SMEM), vmem, vmem],
        out_specs=(pl.BlockSpec(memory_space=pl.ANY), vmem),
        scratch_shapes=[
            pltpu.VMEM((count + 1, HALF, LANES), jnp.bfloat16),
            pltpu.VMEM((outer, *lists.shape), jnp.int32),
            pltpu.SMEM((outer, *lists.shape), jnp.int32),
            pltpu.VMEM((outer, plane_count, slots, HALF, LANES), jnp.bfloat16),
            pltpu.SemaphoreType.DMA,
            pltpu.SemaphoreType.DMA,
            pltpu.SemaphoreType.DMA,
            pltpu.SemaphoreType.DMA((2, outer)),
            pltpu.SemaphoreType.DMA((2, outer)),
            *LineGather.semaphores(outer, 1),
            *[pltpu.VMEM((count + 1, HALF, LANES), jnp.bfloat16)] * (2 * (outer - 1)),
        ],
        compiler_params=pltpu.CompilerParams(
            vmem_limit_bytes=VMEM_LIMIT, collective_id=1, has_side_effects=True
        ),
        name="send_out",
    )(lists, lists, density)


def back_kernel(
    outer, inner, row_count, kept_ref, slots_ref, out_ref,
    landed, wide, total, sums, arriving, land_sem, send_sem, line_send, line_recv
):
    plane = Plane(outer, inner, row_count)
    a, b = plane.a, plane.b
    count = out_ref.shape[0]
    slots = slots_ref.shape[1]
    terms = plane.count * slots
    line = LineGather(None, outer, 1, a, plane.on_line, (None,) * 3)
    plane.greet(line)

    def send_plane(target):
        def one(offset, carry):
            place = plane.peer(offset)
            pltpu.make_async_remote_copy(
                src_ref=slots_ref.at[plane.owner(place, target)],
                dst_ref=landed.at[target, plane.place],
                send_sem=send_sem,
                recv_sem=land_sem.at[target],
                device_id=plane.device(place),
                device_id_type=MESH,
            ).start()
            return carry

        lax.fori_loop(0, plane.count - 1, one, 0)
        pltpu.make_async_copy(
            slots_ref.at[plane.owner(plane.place, target)], landed.at[target, plane.place], land_sem.at[target]
        ).start()

    def combine(target):
        pltpu.make_async_copy(landed.at[target], landed.at[target], land_sem.at[target]).wait()
        wide[...] = landed[target].astype(jnp.float32).reshape(wide.shape)
        numbers = lax.broadcasted_iota(jnp.int32, (count, terms), 0)
        chosen = jnp.where(numbers == kept_ref[pl.ds(target, 1), 0:terms], 1.0, 0.0).astype(jnp.bfloat16)
        for line_at in range(HALF):
            part = wide[pl.ds(line_at, terms, stride=HALF), :].astype(jnp.bfloat16)
            total[pl.ds(line_at, count, stride=HALF), :] = jnp.dot(
                chosen, part, preferred_element_type=jnp.float32
            )

    def wait_line(target, side):
        ref = arriving.at[target, side]
        pltpu.make_async_copy(ref, ref, line_recv.at[target, side]).wait()

    def pass_on(target, step, side):
        return pltpu.make_async_remote_copy(
            src_ref=sums.at[target],
            dst_ref=arriving.at[target, side],
            send_sem=line_send.at[target],
            recv_sem=line_recv.at[target, side],
            device_id=plane.on_line(a + step),
            device_id_type=MESH,
        )

    order = [(d, step) for d in range(outer - 1, 0, -1) for step in (1, -1)] + [(0, 1)]

    def each(d, step, act):
        target = a + d * step

        @pl.when(jnp.logical_and(target >= 0, target < outer))
        def _():
            act(target)

    def nth(k, act):
        far = jnp.maximum(a, outer - 1 - a)
        near = outer - 1 - far
        up = a < outer - 1 - a
        long = far - near
        alone = jnp.where(up, a + far - k, a - far + k)
        rest = k - long
        dist = near - rest // 2
        paired = jnp.where(lax.rem(rest, 2) == 0, a + dist, a - dist)
        act(jnp.where(rest < 0, alone, paired))

    nth(0, send_plane)
    if outer > 1:
        nth(1, send_plane)
    for k in range(outer):

        def handle(target):
            combine(target)
            for side, step in ((0, 1), (1, -1)):

                @pl.when((target - a) * step > 0)
                def _():
                    @pl.when(jnp.logical_and(a - step >= 0, a - step < outer))
                    def _():
                        wait_line(target, side)
                        total[...] += arriving[target, side].astype(jnp.float32).reshape(total.shape)

                    sums[target] = total[...].astype(jnp.bfloat16).reshape(sums.shape[1:])
                    pass_on(target, step, side).start()

        nth(k, handle)
        if k + 2 < outer:
            nth(k + 2, send_plane)
    for side, step in ((0, 1), (1, -1)):

        @pl.when(jnp.logical_and(a - step >= 0, a - step < outer))
        def _():
            wait_line(a, side)
            total[...] += arriving[a, side].astype(jnp.float32).reshape(total.shape)

    out_ref[...] = total[...].reshape(out_ref.shape)
    for d, step in order:
        if d:
            side = 0 if step > 0 else 1
            each(d, step, lambda target: pass_on(target, step, side).wait_send())
    sent = landed.at[:, pl.ds(0, plane.count - 1)]
    pltpu.make_async_copy(sent, sent, send_sem).wait()


def send_blocks_back(lines, count, kept, blocks):
    outer, inner = lines
    row_count = lax.axis_size("row")
    plane_count = row_count * inner
    slots = blocks.shape[1]
    vmem = pl.BlockSpec(memory_space=pltpu.VMEM)
    return pl.pallas_call(
        functools.partial(back_kernel, outer, inner, row_count),
        out_shape=jax.ShapeDtypeStruct((count, HALF, LANES), jnp.float32),
        in_specs=[vmem, pl.BlockSpec(memory_space=pl.ANY)],
        out_specs=vmem,
        scratch_shapes=[
            pltpu.VMEM((outer, plane_count, slots, HALF, LANES), jnp.bfloat16),
            pltpu.VMEM((plane_count * slots * HALF, LANES), jnp.float32),
            pltpu.VMEM((count * HALF, LANES), jnp.float32),
            pltpu.VMEM((outer, count, HALF, LANES), jnp.bfloat16),
            pltpu.VMEM((outer, 2, count, HALF, LANES), jnp.bfloat16),
            pltpu.SemaphoreType.DMA((outer,)),
            pltpu.SemaphoreType.DMA,
            pltpu.SemaphoreType.DMA((outer,)),
            pltpu.SemaphoreType.DMA((outer, 2)),
        ],
        compiler_params=pltpu.CompilerParams(
            vmem_limit_bytes=VMEM_LIMIT, collective_id=2, has_side_effects=True
        ),
        name="send_back",
    )(kept, blocks)


def grid_kernel(chunk, pair_ref, recv_ref, basis_ref, vloc_ref, out_ref, sums, pair_mat, k_all):
    cells = basis_ref.shape[1]
    sums[...] = jnp.zeros_like(sums)
    k_all[...] = jnp.zeros_like(k_all)

    def add_slot(slot, carry):
        at = pair_ref[slot]
        sums[at] = sums[at] + recv_ref[slot].astype(jnp.float32)
        return carry

    lax.fori_loop(0, recv_ref.shape[0], add_slot, 0, unroll=8)

    def assemble(a, carry):
        row = pl.multiple_of(a * EDGE, EDGE)
        for b in range(0, ATOMS, 2):
            top, bottom = join_pair(sums[a * ATOMS + b], sums[a * ATOMS + b + 1])
            lanes = slice(b * EDGE, (b + 2) * EDGE)
            pair_mat[pl.ds(row, HALF), lanes] = top.astype(jnp.bfloat16)
            pair_mat[pl.ds(row + HALF, HALF), lanes] = bottom.astype(jnp.bfloat16)
        return carry

    lax.fori_loop(0, ATOMS, assemble, 0)

    def integrate(step, carry):
        at = pl.ds(pl.multiple_of(step * chunk, chunk), chunk)
        vals = basis_ref[:, at]
        mixed = jnp.dot(pair_mat[...], vals, preferred_element_type=jnp.float32)
        wide = vals.astype(jnp.float32)
        rho = jnp.sum(wide * mixed, axis=0, keepdims=True)
        pot = vloc_ref[:, at] + 0.5 * rho / jnp.sqrt(1.0 + rho * rho)
        weighted = (wide * pot).astype(jnp.bfloat16)
        k_all[...] += lax.dot_general(
            weighted, vals, (((1,), (1,)), ((), ())), preferred_element_type=jnp.float32
        )
        return carry

    lax.fori_loop(0, cells // chunk, integrate, 0)

    def split(a, carry):
        row = pl.multiple_of(a * EDGE, EDGE)
        for b in range(0, ATOMS, 2):
            lanes = slice(b * EDGE, (b + 2) * EDGE)
            first, second = split_pair(k_all[pl.ds(row, HALF), lanes], k_all[pl.ds(row + HALF, HALF), lanes])
            sums[a * ATOMS + b] = first
            sums[a * ATOMS + b + 1] = second
        return carry

    lax.fori_loop(0, ATOMS, split, 0)

    def give_slot(slot, carry):
        out_ref[slot] = sums[pair_ref[slot]].astype(jnp.bfloat16)
        return carry

    lax.fori_loop(0, out_ref.shape[0], give_slot, 0, unroll=8)


def grid_step(pair, received, basis, v_loc):
    order = ATOMS * EDGE
    chunk = math.gcd(basis.shape[1], 512)
    return pl.pallas_call(
        functools.partial(grid_kernel, chunk),
        out_shape=jax.ShapeDtypeStruct(received.shape, jnp.bfloat16),
        in_specs=[pl.BlockSpec(memory_space=pltpu.SMEM)] + [pl.BlockSpec(memory_space=pltpu.VMEM)] * 3,
        out_specs=pl.BlockSpec(memory_space=pltpu.VMEM),
        scratch_shapes=[
            pltpu.VMEM((ATOMS * ATOMS, HALF, LANES), jnp.float32),
            pltpu.VMEM((order, order), jnp.bfloat16),
            pltpu.VMEM((order, order), jnp.float32),
        ],
        compiler_params=pltpu.CompilerParams(vmem_limit_bytes=VMEM_LIMIT),
        name="grid",
    )(pair, received, basis, v_loc)


def block_masks(mask_ref, i, j):
    low = lax.broadcasted_iota(jnp.int32, (EDGE, LANES), 1) < EDGE
    return jnp.where(low, mask_ref[i, j].astype(jnp.float32), mask_ref[i, j + 1].astype(jnp.float32))


def add_kernel(scale, mask_ref, sums, core_ref, ks_ref, x0_ref):
    rows, cols = core_ref.shape
    across = cols // EDGE
    for i in range(rows // EDGE):
        for j in range(0, across, 2):
            lanes = slice(j * EDGE, (j + 2) * EDGE)
            high, mid, low = i * EDGE, i * EDGE + HALF, (i + 1) * EDGE
            top, bottom = join_pair(sums[i * across + j], sums[i * across + j + 1])
            ks_ref[high:mid, lanes] = core_ref[high:mid, lanes] + top
            ks_ref[mid:low, lanes] = core_ref[mid:low, lanes] + bottom
            kept = block_masks(mask_ref, i, j) * ks_ref[high:low, lanes] * scale
            x0_ref[high:low, lanes] = kept.astype(jnp.bfloat16)


def add_back(scale, block_mask, sums, core_ham):
    return pl.pallas_call(
        functools.partial(add_kernel, scale),
        out_shape=(
            jax.ShapeDtypeStruct(core_ham.shape, jnp.float32),
            jax.ShapeDtypeStruct(core_ham.shape, jnp.bfloat16),
        ),
        in_specs=[pl.BlockSpec(memory_space=pltpu.SMEM)] + [pl.BlockSpec(memory_space=pltpu.VMEM)] * 2,
        out_specs=(pl.BlockSpec(memory_space=pltpu.VMEM),) * 2,
        compiler_params=pltpu.CompilerParams(vmem_limit_bytes=VMEM_LIMIT),
        name="add_back",
    )(block_mask, sums, core_ham)


class LineGather:
    def __init__(self, piece, outer, inner, place, device_at, sems):
        self.piece, self.outer, self.inner = piece, outer, inner
        self.a, self.b = place // inner, place % inner
        self.device_at = device_at
        self.out_sem, self.in_sem, self.recv_sem = sems
        self.sent = []

    def neighbours(self):
        a, b = self.a, self.b
        return (
            (a > 0, a - 1, b),
            (a < self.outer - 1, a + 1, b),
            (b > 0, a, b - 1),
            (b < self.inner - 1, a, b + 1),
        )

    def send(self, cond, source, target, sem):
        def describe():
            return pltpu.make_async_remote_copy(
                src_ref=self.piece(source),
                dst_ref=self.piece(source),
                send_sem=sem,
                recv_sem=self.recv_sem.at[source],
                device_id=self.device_at(target),
                device_id_type=MESH,
            )

        @pl.when(cond)
        def _():
            describe().start()

        self.sent.append((cond, describe))

    def arrive(self, source):
        pltpu.make_async_copy(self.piece(source), self.piece(source), self.recv_sem.at[source]).wait()

    def along_inner(self, cond, outer_at, inner_from, step, sem):
        target = self.b + step
        fits = jnp.logical_and(target >= 0, target < self.inner)
        self.send(
            jnp.logical_and(cond, fits), outer_at * self.inner + inner_from, self.a * self.inner + target, sem
        )

    def steps(self):
        a, b, inner = self.a, self.b, self.inner
        for d in range(self.outer):
            for way, step in enumerate((1, -1)):
                if d == 0 and way == 1:
                    have = a >= 0
                    source = a
                else:
                    source = a - d * step
                    have = jnp.logical_and(source >= 0, source < self.outer)
                tile = source * inner + b
                if d > 0:

                    @pl.when(have)
                    def _():
                        self.arrive(tile)

                target = a + step
                fits = jnp.logical_and(target >= 0, target < self.outer)
                self.send(jnp.logical_and(have, fits), tile, target * inner + b, self.out_sem.at[d, way])
                if d > 0 or way == 0:
                    for side, hop in enumerate((1, -1)):
                        self.along_inner(have, source, b, hop, self.in_sem.at[d * 2 + way, side])
            yield
        used = 2 * self.outer
        for e in range(1, inner):
            for outer_at in range(self.outer):
                for way, step in enumerate((1, -1)):
                    origin = b - e * step
                    have = jnp.logical_and(origin >= 0, origin < inner)
                    tile = outer_at * inner + origin

                    @pl.when(have)
                    def _():
                        self.arrive(tile)

                    if e < inner - 1:
                        self.along_inner(have, outer_at, origin, step, self.in_sem.at[used, way])
                if e < inner - 1:
                    used += 1
            yield

    def drain(self):
        for cond, describe in self.sent:

            @pl.when(cond)
            def _():
                describe().wait_send()

    @staticmethod
    def semaphores(outer, inner):
        return [
            pltpu.SemaphoreType.DMA((outer, 2)),
            pltpu.SemaphoreType.DMA((2 * outer + max(inner - 2, 0) * outer, 2)),
            pltpu.SemaphoreType.DMA((outer * inner,)),
        ]


def greet(gathers, others=0):
    barrier = pltpu.get_barrier_semaphore()
    count = others
    for gather in gathers:
        for cond, a, b in gather.neighbours():

            @pl.when(cond)
            def _():
                pl.semaphore_signal(
                    barrier, inc=1, device_id=gather.device_at(a * gather.inner + b), device_id_type=MESH
                )

            count = count + cond.astype(jnp.int32)
    pl.semaphore_wait(barrier, count)


def run_together(*gathers):
    going = [gather.steps() for gather in gathers]
    while going:
        going = [steps for steps in going if next(steps, "end") is None]


def panel_product(left, right, acc):
    height, width = right.shape[1], left.shape[2]
    acc[...] = jnp.zeros_like(acc)
    for j in range(left.shape[0]):
        start = j * width
        part = right[start // height, start % height : start % height + width, :]
        acc[...] += jnp.dot(left[j], part, preferred_element_type=jnp.float32)


def sign_kernel(scale, row_lines, col_lines, mask_ref, x0_ref, out_ref, left, right, second, mask, acc, *sems):
    row, col = lax.axis_index("row"), lax.axis_index("col")
    rows, cols = x0_ref.shape
    along_col = LineGather(left.at.__getitem__, *col_lines, col, lambda at: (row, at), sems[0:3])
    along_row = LineGather(right.at.__getitem__, *row_lines, row, lambda at: (at, col), sems[3:6])
    again = LineGather(second.at.__getitem__, *row_lines, row, lambda at: (at, col), sems[6:9])
    greet([along_col, along_row])
    left[col] = x0_ref[...]
    right[row] = x0_ref[...]
    run_together(along_col, along_row)
    for i in range(rows // EDGE):
        for j in range(0, cols // EDGE, 2):
            mask[i * EDGE : (i + 1) * EDGE, j * EDGE : (j + 2) * EDGE] = block_masks(mask_ref, i, j)
    panel_product(left, right, acc)
    second[row] = (mask[...] * acc[...]).astype(jnp.bfloat16)
    run_together(again)
    panel_product(left, second, acc)
    out_ref[...] = (1.5 * x0_ref[...].astype(jnp.float32) - 0.5 * (mask[...] * acc[...])) / scale
    for gather in (along_col, along_row, again):
        gather.drain()


def sign_step(scale, block_mask, x0):
    row_count, col_count = lax.axis_size("row"), lax.axis_size("col")
    row_lines = (row_count // CORES, CORES)
    outer = math.gcd(col_count, 4)
    col_lines = (outer, col_count // outer)
    rows, cols = x0.shape
    return pl.pallas_call(
        functools.partial(sign_kernel, scale, row_lines, col_lines),
        out_shape=jax.ShapeDtypeStruct(x0.shape, jnp.float32),
        in_specs=[pl.BlockSpec(memory_space=pltpu.SMEM), pl.BlockSpec(memory_space=pltpu.VMEM)],
        out_specs=pl.BlockSpec(memory_space=pltpu.VMEM),
        scratch_shapes=[
            pltpu.VMEM((col_count, rows, cols), jnp.bfloat16),
            pltpu.VMEM((row_count, rows, cols), jnp.bfloat16),
            pltpu.VMEM((row_count, rows, cols), jnp.bfloat16),
            pltpu.VMEM((rows, cols), jnp.float32),
            pltpu.VMEM((rows, cols), jnp.float32),
            *LineGather.semaphores(*col_lines),
            *LineGather.semaphores(*row_lines),
            *LineGather.semaphores(*row_lines),
        ],
        compiler_params=pltpu.CompilerParams(
            vmem_limit_bytes=VMEM_LIMIT, collective_id=0, has_side_effects=True
        ),
        name="sign",
    )(block_mask, x0)


def body(density, core_ham, block_mask, send_blocks, task_atoms, basis, v_loc):
    row_count, col_count = lax.axis_size("row"), lax.axis_size("col")
    block_rows = density.shape[0] // EDGE
    local_count = block_rows * (density.shape[1] // EDGE)
    capacity = send_blocks.shape[2]
    outer = math.gcd(col_count, 4)
    inner = col_count // outer
    slots = send_blocks[0].reshape(row_count, outer, inner * capacity)
    lists = jnp.where(slots >= 0, slots, local_count).transpose(1, 0, 2).reshape(outer, -1)
    lists = jnp.pad(lists, ((0, -outer % 8), (0, -lists.shape[1] % 128)))
    atoms = task_atoms[:, 0]
    pair = (atoms[0] * ATOMS + atoms[1]).reshape(-1)
    received, kept = send_blocks_out((outer, inner), capacity, lists, density)
    k_slot = grid_step(pair, received.reshape(-1, HALF, LANES), basis[0], v_loc)
    sums = send_blocks_back((outer, inner), local_count, kept, k_slot.reshape(received.shape))
    scale = 1.0 / math.sqrt(16.0 * block_rows * row_count)
    ks_matrix, x0 = add_back(scale, block_mask, sums, core_ham)
    return (ks_matrix, sign_step(scale, block_mask, x0))


def solution(mesh):
    placed = (
        P("row", "col"),
        P("row", "col"),
        P("row", "col"),
        P(("row", "col"), None, None),
        P(None, ("row", "col"), None, None),
        P(("row", "col"), None, None),
        P(("row", "col"), None),
    )
    return jax.shard_map(
        body,
        mesh=mesh,
        in_specs=placed,
        out_specs=(P("row", "col"), P("row", "col")),
        check_vma=False,
    )
```

```python
import functools
import math

import jax
import jax.numpy as jnp
from jax import lax
from jax.experimental import pallas as pl
from jax.experimental.pallas import tpu as pltpu
from jax.sharding import PartitionSpec as P

ATOMS = 16
EDGE = 64
HALF = EDGE // 2
LANES = 2 * EDGE
CORES = 2
MESH = pl.DeviceIdType.MESH
VMEM_LIMIT = 56 * 1024 * 1024


def low_lanes():
    return lax.broadcasted_iota(jnp.int32, (HALF, LANES), 1) < EDGE


def join_pair(first, second):
    low = low_lanes()
    top = jnp.where(low, first, pltpu.roll(second, EDGE, 1))
    bottom = jnp.where(low, pltpu.roll(first, EDGE, 1), second)
    return top, bottom


def split_pair(top, bottom):
    return join_pair(top, bottom)


class Plane:
    def __init__(self, outer, inner, row_count):
        self.outer, self.inner, self.count = outer, inner, row_count * inner
        self.row, col = lax.axis_index("row"), lax.axis_index("col")
        self.a, self.b = col // inner, col % inner
        self.place = self.row * inner + self.b

    def peer(self, offset):
        return lax.rem(self.place + 1 + offset, self.count)

    def device(self, place):
        return (place // self.inner, self.a * self.inner + place % self.inner)

    def owner(self, place, outer_at):
        return (place // self.inner) * (self.outer * self.inner) + outer_at * self.inner + place % self.inner

    def on_line(self, outer_at):
        return (self.row, outer_at * self.inner + self.b)

    def greet(self, line):
        barrier = pltpu.get_barrier_semaphore()

        def signal(offset, carry):
            pl.semaphore_signal(barrier, inc=1, device_id=self.device(self.peer(offset)), device_id_type=MESH)
            return carry

        lax.fori_loop(0, self.count - 1, signal, 0)
        greet([line], self.count - 1)


def send_kernel(
    outer, inner, row_count, index_ref, lists_ref, density_ref, out_ref, kept_ref,
    own, lists, lists_smem, stage, list_sem, recv_sem, send_sem, tile_send, tile_recv, *rest
):
    plane = Plane(outer, inner, row_count)
    a = plane.a
    rows, cols = density_ref.shape
    across = cols // EDGE
    count = (rows // EDGE) * across
    slots = stage.shape[2]
    entries = LineGather(lists.at.__getitem__, outer, 1, a, plane.on_line, rest[0:3])
    arrived = (rest[3 : 2 + outer], rest[2 + outer :])
    for tile in (own, *arrived[0], *arrived[1]):
        tile[count] = jnp.zeros((HALF, LANES), tile.dtype)
    plane.greet(entries)
    lists[a] = lists_ref[...]
    for i in range(rows // EDGE):
        for j in range(0, across, 2):
            lanes = slice(j * EDGE, (j + 2) * EDGE)
            top = density_ref[i * EDGE : i * EDGE + HALF, lanes].astype(jnp.float32)
            bottom = density_ref[i * EDGE + HALF : (i + 1) * EDGE, lanes].astype(jnp.float32)
            first, second = split_pair(top, bottom)
            own[i * across + j] = first.astype(own.dtype)
            own[i * across + j + 1] = second.astype(own.dtype)

    def passes(d, step):
        source, target = a - d * step, a + step
        return jnp.logical_and(
            jnp.logical_and(source >= 0, source < outer), jnp.logical_and(target >= 0, target < outer)
        )

    def pass_on(d, way, step):
        tile = arrived[way][d - 1] if d else own
        return pltpu.make_async_remote_copy(
            src_ref=tile.at[pl.ds(0, count)],
            dst_ref=arrived[way][d].at[pl.ds(0, count)],
            send_sem=tile_send.at[way, d],
            recv_sem=tile_recv.at[way, d],
            device_id=plane.on_line(a + step),
            device_id_type=MESH,
        )

    def serve(tile, source, number):
        def pick(offset, place):
            for slot in range(slots):
                stage[source, offset, slot] = tile[number(place * slots + slot)]

        def one(offset, carry):
            place = plane.peer(offset)
            pick(offset, place)
            pltpu.make_async_remote_copy(
                src_ref=stage.at[source, offset],
                dst_ref=out_ref.at[plane.owner(plane.place, source)],
                send_sem=send_sem,
                recv_sem=recv_sem,
                device_id=plane.device(place),
                device_id_type=MESH,
            ).start()
            return carry

        lax.fori_loop(0, plane.count - 1, one, 0)
        pick(plane.count - 1, plane.place)
        pltpu.make_async_copy(
            stage.at[source, plane.count - 1], out_ref.at[plane.owner(plane.place, source)], recv_sem
        ).start()

    entry_steps = entries.steps()
    for d in range(outer):
        next(entry_steps)
        if d:
            for way, step in enumerate((1, -1)):

                @pl.when(jnp.logical_and(a - d * step >= 0, a - d * step < outer))
                def _():
                    tile = arrived[way][d - 1].at[pl.ds(0, count)]
                    pltpu.make_async_copy(tile, tile, tile_recv.at[way, d - 1]).wait()

        if d < outer - 1:
            for way, step in enumerate((1, -1)):

                @pl.when(passes(d, step))
                def _():
                    pass_on(d, way, step).start()

        if d == 0:
            serve(own, a, lambda at: index_ref[a, at])
            continue
        for way, step in enumerate((1, -1)):
            source = a - d * step

            @pl.when(jnp.logical_and(source >= 0, source < outer))
            def _():
                copy = pltpu.make_async_copy(lists.at[source], lists_smem.at[source], list_sem)
                copy.start()
                copy.wait()
                serve(arrived[way][d - 1], source, lambda at: lists_smem[source, a, at])

    kept_ref[...] = jnp.zeros_like(kept_ref)
    for i in range(outer):
        kept_ref[i : i + 1, :] = lists[i, pl.ds(a, 1), :]
    for d in range(outer - 1):
        for way, step in enumerate((1, -1)):

            @pl.when(passes(d, step))
            def _():
                pass_on(d, way, step).wait_send()

    entries.drain()
    sent = stage.at[:, pl.ds(0, plane.count - 1)]
    pltpu.make_async_copy(sent, sent, send_sem).wait()
    pltpu.make_async_copy(out_ref, out_ref, recv_sem).wait()


def send_blocks_out(lines, slots, lists, density):
    outer, inner = lines
    row_count, col_count = lax.axis_size("row"), lax.axis_size("col")
    plane_count = row_count * inner
    count = (density.shape[0] // EDGE) * (density.shape[1] // EDGE)
    vmem = pl.BlockSpec(memory_space=pltpu.VMEM)
    return pl.pallas_call(
        functools.partial(send_kernel, outer, inner, row_count),
        out_shape=(
            jax.ShapeDtypeStruct((row_count * col_count, slots, HALF, LANES), jnp.bfloat16),
            jax.ShapeDtypeStruct(lists.shape, jnp.int32),
        ),
        in_specs=[pl.BlockSpec(memory_space=pltpu.SMEM), vmem, vmem],
        out_specs=(pl.BlockSpec(memory_space=pl.ANY), vmem),
        scratch_shapes=[
            pltpu.VMEM((count + 1, HALF, LANES), jnp.bfloat16),
            pltpu.VMEM((outer, *lists.shape), jnp.int32),
            pltpu.SMEM((outer, *lists.shape), jnp.int32),
            pltpu.VMEM((outer, plane_count, slots, HALF, LANES), jnp.bfloat16),
            pltpu.SemaphoreType.DMA,
            pltpu.SemaphoreType.DMA,
            pltpu.SemaphoreType.DMA,
            pltpu.SemaphoreType.DMA((2, outer)),
            pltpu.SemaphoreType.DMA((2, outer)),
            *LineGather.semaphores(outer, 1),
            *[pltpu.VMEM((count + 1, HALF, LANES), jnp.bfloat16)] * (2 * (outer - 1)),
        ],
        compiler_params=pltpu.CompilerParams(
            vmem_limit_bytes=VMEM_LIMIT, collective_id=1, has_side_effects=True
        ),
        name="send_out",
    )(lists, lists, density)


def back_kernel(
    scale, outer, inner, row_count, kept_ref, mask_ref, slots_ref, core_ref, ham_ref, x0_ref, x3_ref,
    landed, wide, total, sums, arriving, land_sem, send_sem, line_send, line_recv, *rest
):
    plane = Plane(outer, inner, row_count)
    a, b = plane.a, plane.b
    rows, cols = core_ref.shape
    across = cols // EDGE
    count = sums.shape[1]
    slots = slots_ref.shape[1]
    terms = plane.count * slots
    line = LineGather(None, outer, 1, a, plane.on_line, (None,) * 3)
    plane.greet(line)

    def send_plane(target):
        def one(offset, carry):
            place = plane.peer(offset)
            pltpu.make_async_remote_copy(
                src_ref=slots_ref.at[plane.owner(place, target)],
                dst_ref=landed.at[target, plane.place],
                send_sem=send_sem.at[target],
                recv_sem=land_sem.at[target],
                device_id=plane.device(place),
                device_id_type=MESH,
            ).start()
            return carry

        lax.fori_loop(0, plane.count - 1, one, 0)
        pltpu.make_async_copy(
            slots_ref.at[plane.owner(plane.place, target)], landed.at[target, plane.place], land_sem.at[target]
        ).start()

    def combine(target):
        pltpu.make_async_copy(landed.at[target], landed.at[target], land_sem.at[target]).wait()
        wide[...] = landed[target].astype(jnp.float32).reshape(wide.shape)
        numbers = lax.broadcasted_iota(jnp.int32, (count, terms), 0)
        chosen = jnp.where(numbers == kept_ref[pl.ds(target, 1), 0:terms], 1.0, 0.0).astype(jnp.bfloat16)
        for line_at in range(HALF):
            part = wide[pl.ds(line_at, terms, stride=HALF), :].astype(jnp.bfloat16)
            total[pl.ds(line_at, count, stride=HALF), :] = jnp.dot(
                chosen, part, preferred_element_type=jnp.float32
            )

    def wait_line(target, side):
        ref = arriving.at[target, side]
        pltpu.make_async_copy(ref, ref, line_recv.at[target, side]).wait()

    def pass_on(target, step, side):
        return pltpu.make_async_remote_copy(
            src_ref=sums.at[target],
            dst_ref=arriving.at[target, side],
            send_sem=line_send.at[target],
            recv_sem=line_recv.at[target, side],
            device_id=plane.on_line(a + step),
            device_id_type=MESH,
        )

    order = [(d, step) for d in range(outer - 1, 0, -1) for step in (1, -1)] + [(0, 1)]

    def each(d, step, act):
        target = a + d * step

        @pl.when(jnp.logical_and(target >= 0, target < outer))
        def _():
            act(target)

    def nth(k, act):
        far = jnp.maximum(a, outer - 1 - a)
        near = outer - 1 - far
        up = a < outer - 1 - a
        long = far - near
        alone = jnp.where(up, a + far - k, a - far + k)
        rest = k - long
        dist = near - rest // 2
        paired = jnp.where(lax.rem(rest, 2) == 0, a + dist, a - dist)
        act(jnp.where(rest < 0, alone, paired))

    def sent_plane(target):
        sent = landed.at[target, pl.ds(0, plane.count - 1)]
        pltpu.make_async_copy(sent, sent, send_sem.at[target]).wait()

    nth(0, send_plane)
    for k in range(outer):
        nth(k, sent_plane)
        if k + 1 < outer:
            nth(k + 1, send_plane)

        def handle(target):
            combine(target)
            for side, step in ((0, 1), (1, -1)):

                @pl.when((target - a) * step > 0)
                def _():
                    @pl.when(jnp.logical_and(a - step >= 0, a - step < outer))
                    def _():
                        wait_line(target, side)
                        total[...] += arriving[target, side].astype(jnp.float32).reshape(total.shape)

                    sums[target] = total[...].astype(jnp.bfloat16).reshape(sums.shape[1:])
                    pass_on(target, step, side).start()

        nth(k, handle)
    for side, step in ((0, 1), (1, -1)):

        @pl.when(jnp.logical_and(a - step >= 0, a - step < outer))
        def _():
            wait_line(a, side)
            total[...] += arriving[a, side].astype(jnp.float32).reshape(total.shape)

    for i in range(rows // EDGE):
        for j in range(0, across, 2):
            lanes = slice(j * EDGE, (j + 2) * EDGE)
            high, mid, low = i * EDGE, i * EDGE + HALF, (i + 1) * EDGE
            at = (i * across + j) * HALF
            top, bottom = join_pair(total[at : at + HALF, :], total[at + HALF : at + 2 * HALF, :])
            ham_ref[high:mid, lanes] = top
            ham_ref[mid:low, lanes] = bottom
            ks = core_ref[high:low, lanes] + ham_ref[high:low, lanes]
            x0_ref[high:low, lanes] = (block_masks(mask_ref, i, j) * ks * scale).astype(jnp.bfloat16)

    sign_part(plane, mask_ref, x0_ref, x3_ref, *rest)
    for d, step in order:
        if d:
            side = 0 if step > 0 else 1
            each(d, step, lambda target: pass_on(target, step, side).wait_send())


def send_blocks_back(scale, lines, kept, blocks, block_mask, core_ham):
    outer, inner = lines
    row_count, col_count = lax.axis_size("row"), lax.axis_size("col")
    row_lines = (row_count // CORES, CORES)
    plane_count = row_count * inner
    slots = blocks.shape[1]
    rows, cols = core_ham.shape
    count = (rows // EDGE) * (cols // EDGE)
    vmem = pl.BlockSpec(memory_space=pltpu.VMEM)
    return pl.pallas_call(
        functools.partial(back_kernel, scale, outer, inner, row_count),
        out_shape=(
            jax.ShapeDtypeStruct(core_ham.shape, jnp.float32),
            jax.ShapeDtypeStruct(core_ham.shape, jnp.bfloat16),
            jax.ShapeDtypeStruct(core_ham.shape, jnp.float32),
        ),
        in_specs=[vmem, vmem, pl.BlockSpec(memory_space=pl.ANY), vmem],
        out_specs=(vmem,) * 3,
        scratch_shapes=[
            pltpu.VMEM((outer, plane_count, slots, HALF, LANES), jnp.bfloat16),
            pltpu.VMEM((plane_count * slots * HALF, LANES), jnp.float32),
            pltpu.VMEM((count * HALF, LANES), jnp.float32),
            pltpu.VMEM((outer, count, HALF, LANES), jnp.bfloat16),
            pltpu.VMEM((outer, 2, count, HALF, LANES), jnp.bfloat16),
            pltpu.SemaphoreType.DMA((outer,)),
            pltpu.SemaphoreType.DMA((outer,)),
            pltpu.SemaphoreType.DMA((outer,)),
            pltpu.SemaphoreType.DMA((outer, 2)),
            pltpu.VMEM((col_count, rows, cols), jnp.bfloat16),
            pltpu.VMEM((row_count, rows, cols), jnp.bfloat16),
            pltpu.VMEM((row_count, rows, cols), jnp.bfloat16),
            pltpu.VMEM((rows, cols), jnp.float32),
            pltpu.VMEM((rows, cols), jnp.float32),
            *LineGather.semaphores(outer, inner),
            *LineGather.semaphores(inner, outer),
            *LineGather.semaphores(*row_lines),
            *LineGather.semaphores(*row_lines),
        ],
        compiler_params=pltpu.CompilerParams(
            vmem_limit_bytes=VMEM_LIMIT, collective_id=2, has_side_effects=True
        ),
        name="back_and_sign",
    )(kept, block_mask, blocks, core_ham)


def grid_kernel(
    chunk, pair_ref, recv_ref, basis_hbm, vloc_ref, out_ref, sums, pair_mat, k_all, basis_ref, weighted, sem
):
    cells = basis_ref.shape[1]
    load = pltpu.make_async_copy(basis_hbm, basis_ref, sem)
    load.start()
    sums[...] = jnp.zeros_like(sums)

    def add_slot(slot, carry):
        at = pair_ref[slot]
        sums[at] = sums[at] + recv_ref[slot].astype(jnp.float32)
        return carry

    lax.fori_loop(0, recv_ref.shape[0], add_slot, 0, unroll=8)

    def assemble(a, carry):
        row = pl.multiple_of(a * EDGE, EDGE)
        for b in range(0, ATOMS, 2):
            top, bottom = join_pair(sums[a * ATOMS + b], sums[a * ATOMS + b + 1])
            lanes = slice(b * EDGE, (b + 2) * EDGE)
            pair_mat[pl.ds(row, HALF), lanes] = top.astype(jnp.bfloat16)
            pair_mat[pl.ds(row + HALF, HALF), lanes] = bottom.astype(jnp.bfloat16)
        return carry

    lax.fori_loop(0, ATOMS, assemble, 0)
    load.wait()

    def integrate(step, carry):
        at = pl.ds(pl.multiple_of(step * chunk, chunk), chunk)
        vals = basis_ref[:, at]
        mixed = jnp.dot(pair_mat[...], vals, preferred_element_type=jnp.float32)
        wide = vals.astype(jnp.float32)
        rho = jnp.sum(wide * mixed, axis=0, keepdims=True)
        pot = vloc_ref[:, at] + 0.5 * rho / jnp.sqrt(1.0 + rho * rho)
        weighted[:, at] = (wide * pot).astype(jnp.bfloat16)
        return carry

    lax.fori_loop(0, cells // chunk, integrate, 0)
    columns = 4 * EDGE

    def multiply(step, carry):
        at = pl.ds(pl.multiple_of(step * columns, columns), columns)
        k_all[:, at] = lax.dot_general(
            weighted[...], basis_ref[at, :], (((1,), (1,)), ((), ())), preferred_element_type=jnp.float32
        )
        return carry

    lax.fori_loop(0, k_all.shape[1] // columns, multiply, 0)

    def split(a, carry):
        row = pl.multiple_of(a * EDGE, EDGE)
        for b in range(0, ATOMS, 2):
            lanes = slice(b * EDGE, (b + 2) * EDGE)
            first, second = split_pair(k_all[pl.ds(row, HALF), lanes], k_all[pl.ds(row + HALF, HALF), lanes])
            sums[a * ATOMS + b] = first
            sums[a * ATOMS + b + 1] = second
        return carry

    lax.fori_loop(0, ATOMS, split, 0)

    def give_slot(slot, carry):
        out_ref[slot] = sums[pair_ref[slot]].astype(jnp.bfloat16)
        return carry

    lax.fori_loop(0, out_ref.shape[0], give_slot, 0, unroll=8)


def grid_step(pair, received, basis, v_loc):
    order = ATOMS * EDGE
    chunk = math.gcd(basis.shape[1], 512)
    return pl.pallas_call(
        functools.partial(grid_kernel, chunk),
        out_shape=jax.ShapeDtypeStruct(received.shape, jnp.bfloat16),
        in_specs=[
            pl.BlockSpec(memory_space=pltpu.SMEM),
            pl.BlockSpec(memory_space=pltpu.VMEM),
            pl.BlockSpec(memory_space=pl.ANY),
            pl.BlockSpec(memory_space=pltpu.VMEM),
        ],
        out_specs=pl.BlockSpec(memory_space=pltpu.VMEM),
        scratch_shapes=[
            pltpu.VMEM((ATOMS * ATOMS, HALF, LANES), jnp.float32),
            pltpu.VMEM((order, order), jnp.bfloat16),
            pltpu.VMEM((order, order), jnp.float32),
            pltpu.VMEM(basis.shape, jnp.bfloat16),
            pltpu.VMEM(basis.shape, jnp.bfloat16),
            pltpu.SemaphoreType.DMA,
        ],
        compiler_params=pltpu.CompilerParams(vmem_limit_bytes=VMEM_LIMIT),
        name="grid",
    )(pair, received, basis, v_loc)


def block_masks(mask_ref, i, j):
    low = lax.broadcasted_iota(jnp.int32, (EDGE, LANES), 1) < EDGE
    left, right = mask_ref[i : i + 1, j : j + 1], mask_ref[i : i + 1, j + 1 : j + 2]
    return jnp.where(low, left.astype(jnp.float32), right.astype(jnp.float32))


class LineGather:
    def __init__(self, piece, outer, inner, place, device_at, sems):
        self.piece, self.outer, self.inner = piece, outer, inner
        self.a, self.b = place // inner, place % inner
        self.device_at = device_at
        self.out_sem, self.in_sem, self.recv_sem = sems
        self.sent = []

    def neighbours(self):
        a, b = self.a, self.b
        return (
            (a > 0, a - 1, b),
            (a < self.outer - 1, a + 1, b),
            (b > 0, a, b - 1),
            (b < self.inner - 1, a, b + 1),
        )

    def send(self, cond, source, target, sem):
        def describe():
            return pltpu.make_async_remote_copy(
                src_ref=self.piece(source),
                dst_ref=self.piece(source),
                send_sem=sem,
                recv_sem=self.recv_sem.at[source],
                device_id=self.device_at(target),
                device_id_type=MESH,
            )

        @pl.when(cond)
        def _():
            describe().start()

        self.sent.append((cond, describe))

    def arrive(self, source):
        pltpu.make_async_copy(self.piece(source), self.piece(source), self.recv_sem.at[source]).wait()

    def along_inner(self, cond, outer_at, inner_from, step, sem):
        target = self.b + step
        fits = jnp.logical_and(target >= 0, target < self.inner)
        self.send(
            jnp.logical_and(cond, fits), outer_at * self.inner + inner_from, self.a * self.inner + target, sem
        )

    def begin(self):
        self.going = self.steps()
        next(self.going)

    def steps(self):
        a, b, inner = self.a, self.b, self.inner
        for d in range(self.outer):
            for way, step in enumerate((1, -1)):
                if d == 0 and way == 1:
                    have = a >= 0
                    source = a
                else:
                    source = a - d * step
                    have = jnp.logical_and(source >= 0, source < self.outer)
                tile = source * inner + b
                if d > 0:

                    @pl.when(have)
                    def _():
                        self.arrive(tile)

                target = a + step
                fits = jnp.logical_and(target >= 0, target < self.outer)
                self.send(jnp.logical_and(have, fits), tile, target * inner + b, self.out_sem.at[d, way])
                if d > 0 or way == 0:
                    for side, hop in enumerate((1, -1)):
                        self.along_inner(have, source, b, hop, self.in_sem.at[d * 2 + way, side])
            yield
        used = 2 * self.outer
        for e in range(1, inner):
            for outer_at in range(self.outer):
                for way, step in enumerate((1, -1)):
                    origin = b - e * step
                    have = jnp.logical_and(origin >= 0, origin < inner)
                    tile = outer_at * inner + origin

                    @pl.when(have)
                    def _():
                        self.arrive(tile)

                    if e < inner - 1:
                        self.along_inner(have, outer_at, origin, step, self.in_sem.at[used, way])
                if e < inner - 1:
                    used += 1
            yield

    def drain(self):
        for cond, describe in self.sent:

            @pl.when(cond)
            def _():
                describe().wait_send()

    @staticmethod
    def semaphores(outer, inner):
        return [
            pltpu.SemaphoreType.DMA((outer, 2)),
            pltpu.SemaphoreType.DMA((2 * outer + max(inner - 2, 0) * outer, 2)),
            pltpu.SemaphoreType.DMA((outer * inner,)),
        ]


def greet(gathers, others=0):
    barrier = pltpu.get_barrier_semaphore()
    count = others
    for gather in gathers:
        for cond, a, b in gather.neighbours():

            @pl.when(cond)
            def _():
                pl.semaphore_signal(
                    barrier, inc=1, device_id=gather.device_at(a * gather.inner + b), device_id_type=MESH
                )

            count = count + cond.astype(jnp.int32)
    pl.semaphore_wait(barrier, count)


def run_together(*gathers):
    going = [gather.going for gather in gathers]
    while going:
        going = [steps for steps in going if next(steps, "end") is None]


def add_product(acc, left, right, place):
    width = left.shape[2]
    share = right.shape[1] // width
    for part in range(share):
        piece = right[place, part * width : (part + 1) * width, :]
        acc[...] += jnp.dot(left[place * share + part], piece, preferred_element_type=jnp.float32)


def first_rows(rows, outer, inner):
    if inner == 1 or outer == 1:
        return rows
    share = ((outer - 1) * inner - (inner - 1)) / (2 * (outer - 1) * (inner - 1))
    return min(rows - 16, max(16, round(share * rows / 16) * 16))


def sign_part(plane, mask_ref, x0_ref, x3_ref, left, right, second, mask, acc, *sems):
    row, outer, inner = plane.row, plane.outer, plane.inner
    col = plane.a * inner + plane.b
    rows, cols = x0_ref.shape
    row_lines = (right.shape[0] // CORES, CORES)
    split = first_rows(rows, outer, inner)

    def turned(at):
        return (at % outer) * inner + at // outer

    gathers = [
        LineGather(
            lambda at: left.at[at, pl.ds(0, split)], outer, inner, col, lambda at: (row, at), sems[0:3]
        ),
        LineGather(right.at.__getitem__, *row_lines, row, lambda at: (at, col), sems[6:9]),
    ]
    if split < rows:
        gathers.insert(
            1,
            LineGather(
                lambda at: left.at[turned(at), pl.ds(split, rows - split)],
                inner,
                outer,
                plane.b * outer + plane.a,
                lambda at: (row, turned(at)),
                sems[3:6],
            ),
        )
    again = LineGather(second.at.__getitem__, *row_lines, row, lambda at: (at, col), sems[9:12])
    left[col] = x0_ref[...]
    right[row] = x0_ref[...]
    for gather in gathers:
        gather.begin()
    for i in range(rows // EDGE):
        for j in range(0, cols // EDGE, 2):
            mask[i * EDGE : (i + 1) * EDGE, j * EDGE : (j + 2) * EDGE] = block_masks(mask_ref, i, j)
    run_together(*gathers)
    acc[...] = jnp.zeros_like(acc)
    for place in range(right.shape[0]):
        add_product(acc, left, right, place)
    second[row] = (mask[...] * acc[...]).astype(jnp.bfloat16)
    again.begin()
    acc[...] = jnp.zeros_like(acc)
    add_product(acc, left, second, row)
    run_together(again)
    for offset in range(1, right.shape[0]):
        add_product(acc, left, second, lax.rem(row + offset, right.shape[0]))
    x3_ref[...] = mask[...] * acc[...]
    for gather in (*gathers, again):
        gather.drain()


def body(density, core_ham, block_mask, send_blocks, task_atoms, basis, v_loc):
    row_count, col_count = lax.axis_size("row"), lax.axis_size("col")
    block_rows = density.shape[0] // EDGE
    local_count = block_rows * (density.shape[1] // EDGE)
    capacity = send_blocks.shape[2]
    outer = math.gcd(col_count, 4)
    inner = col_count // outer
    slots = send_blocks[0].reshape(row_count, outer, inner * capacity)
    lists = jnp.where(slots >= 0, slots, local_count).transpose(1, 0, 2).reshape(outer, -1)
    lists = jnp.pad(lists, ((0, -outer % 8), (0, -lists.shape[1] % 128)))
    atoms = task_atoms[:, 0]
    pair = (atoms[0] * ATOMS + atoms[1]).reshape(-1)
    received, kept = send_blocks_out((outer, inner), capacity, lists, density)
    k_slot = grid_step(pair, received.reshape(-1, HALF, LANES), basis[0], v_loc)
    scale = 1.0 / math.sqrt(16.0 * block_rows * row_count)
    ham_tile, x0, x3 = send_blocks_back(
        scale, (outer, inner), kept, k_slot.reshape(received.shape), block_mask, core_ham
    )
    return (core_ham + ham_tile, (1.5 * x0.astype(jnp.float32) - 0.5 * x3) / scale)


def solution(mesh):
    placed = (
        P("row", "col"),
        P("row", "col"),
        P("row", "col"),
        P(("row", "col"), None, None),
        P(None, ("row", "col"), None, None),
        P(("row", "col"), None, None),
        P(("row", "col"), None),
    )
    return jax.shard_map(
        body,
        mesh=mesh,
        in_specs=placed,
        out_specs=(P("row", "col"), P("row", "col")),
        check_vma=False,
    )
```

```python
import functools
import math

import jax
import jax.numpy as jnp
from jax import lax
from jax.experimental import pallas as pl
from jax.experimental.pallas import tpu as pltpu
from jax.sharding import PartitionSpec as P

ATOMS = 16
EDGE = 64
HALF = EDGE // 2
LANES = 2 * EDGE
CORES = 2
MESH = pl.DeviceIdType.MESH
VMEM_LIMIT = 56 * 1024 * 1024


def low_lanes():
    return lax.broadcasted_iota(jnp.int32, (HALF, LANES), 1) < EDGE


def join_pair(first, second):
    low = low_lanes()
    top = jnp.where(low, first, pltpu.roll(second, EDGE, 1))
    bottom = jnp.where(low, pltpu.roll(first, EDGE, 1), second)
    return top, bottom


def split_pair(top, bottom):
    return join_pair(top, bottom)


class Plane:
    def __init__(self, outer, inner, row_count):
        self.outer, self.inner, self.count = outer, inner, row_count * inner
        self.row, col = lax.axis_index("row"), lax.axis_index("col")
        self.a, self.b = col // inner, col % inner
        self.place = self.row * inner + self.b

    def peer(self, offset):
        return lax.rem(self.place + 1 + offset, self.count)

    def device(self, place):
        return (place // self.inner, self.a * self.inner + place % self.inner)

    def owner(self, place, outer_at):
        return (place // self.inner) * (self.outer * self.inner) + outer_at * self.inner + place % self.inner

    def on_line(self, outer_at):
        return (self.row, outer_at * self.inner + self.b)

    def greet(self, line):
        barrier = pltpu.get_barrier_semaphore()

        def signal(offset, carry):
            pl.semaphore_signal(barrier, inc=1, device_id=self.device(self.peer(offset)), device_id_type=MESH)
            return carry

        lax.fori_loop(0, self.count - 1, signal, 0)
        greet([line], self.count - 1)


def send_kernel(
    outer, inner, row_count, index_ref, lists_ref, density_ref, out_ref, kept_ref,
    own, lists, lists_smem, stage, list_sem, recv_sem, send_sem, tile_send, tile_recv, *rest
):
    plane = Plane(outer, inner, row_count)
    a = plane.a
    rows, cols = density_ref.shape
    across = cols // EDGE
    count = (rows // EDGE) * across
    slots = stage.shape[2]
    entries = LineGather(lists.at.__getitem__, outer, 1, a, plane.on_line, rest[0:3])
    arrived = (rest[3 : 2 + outer], rest[2 + outer :])
    for tile in (own, *arrived[0], *arrived[1]):
        tile[count] = jnp.zeros((HALF, LANES), tile.dtype)
    plane.greet(entries)
    lists[a] = jnp.zeros(lists.shape[1:], jnp.int32)
    lists[a, 0 : lists_ref.shape[0], 0 : lists_ref.shape[1]] = lists_ref[...]
    for i in range(rows // EDGE):
        for j in range(0, across, 2):
            lanes = slice(j * EDGE, (j + 2) * EDGE)
            top = density_ref[i * EDGE : i * EDGE + HALF, lanes].astype(jnp.float32)
            bottom = density_ref[i * EDGE + HALF : (i + 1) * EDGE, lanes].astype(jnp.float32)
            first, second = split_pair(top, bottom)
            own[i * across + j] = first.astype(own.dtype)
            own[i * across + j + 1] = second.astype(own.dtype)

    def passes(d, step):
        source, target = a - d * step, a + step
        return jnp.logical_and(
            jnp.logical_and(source >= 0, source < outer), jnp.logical_and(target >= 0, target < outer)
        )

    def pass_on(d, way, step):
        tile = arrived[way][d - 1] if d else own
        return pltpu.make_async_remote_copy(
            src_ref=tile.at[pl.ds(0, count)],
            dst_ref=arrived[way][d].at[pl.ds(0, count)],
            send_sem=tile_send.at[way, d],
            recv_sem=tile_recv.at[way, d],
            device_id=plane.on_line(a + step),
            device_id_type=MESH,
        )

    def serve(tile, source, number):
        def pick(offset, place):
            target = plane.owner(place, a)
            for slot in range(slots):
                found = number(slot, target)
                local = jnp.where(found >= 0, found, count)
                stage[source, offset, slot] = tile[local]
                kept_ref[source, place * slots + slot] = local

        def one(offset, carry):
            place = plane.peer(offset)
            pick(offset, place)
            pltpu.make_async_remote_copy(
                src_ref=stage.at[source, offset],
                dst_ref=out_ref.at[plane.owner(plane.place, source)],
                send_sem=send_sem,
                recv_sem=recv_sem,
                device_id=plane.device(place),
                device_id_type=MESH,
            ).start()
            return carry

        lax.fori_loop(0, plane.count - 1, one, 0)
        pick(plane.count - 1, plane.place)
        pltpu.make_async_copy(
            stage.at[source, plane.count - 1], out_ref.at[plane.owner(plane.place, source)], recv_sem
        ).start()

    entry_steps = entries.steps()
    for d in range(outer):
        next(entry_steps)
        if d:
            for way, step in enumerate((1, -1)):

                @pl.when(jnp.logical_and(a - d * step >= 0, a - d * step < outer))
                def _():
                    tile = arrived[way][d - 1].at[pl.ds(0, count)]
                    pltpu.make_async_copy(tile, tile, tile_recv.at[way, d - 1]).wait()

        if d < outer - 1:
            for way, step in enumerate((1, -1)):

                @pl.when(passes(d, step))
                def _():
                    pass_on(d, way, step).start()

        if d == 0:
            serve(own, a, lambda slot, at: index_ref[slot, at])
            continue
        for way, step in enumerate((1, -1)):
            source = a - d * step

            @pl.when(jnp.logical_and(source >= 0, source < outer))
            def _():
                copy = pltpu.make_async_copy(lists.at[source], lists_smem.at[source], list_sem)
                copy.start()
                copy.wait()
                serve(arrived[way][d - 1], source, lambda slot, at: lists_smem[source, slot, at])

    for d in range(outer - 1):
        for way, step in enumerate((1, -1)):

            @pl.when(passes(d, step))
            def _():
                pass_on(d, way, step).wait_send()

    entries.drain()
    sent = stage.at[:, pl.ds(0, plane.count - 1)]
    pltpu.make_async_copy(sent, sent, send_sem).wait()
    pltpu.make_async_copy(out_ref, out_ref, recv_sem).wait()


def up_to(size, step):
    return size + -size % step


def send_blocks_out(lines, lists, density):
    outer, inner = lines
    slots, devices = lists.shape
    row_count, col_count = lax.axis_size("row"), lax.axis_size("col")
    plane_count = row_count * inner
    count = (density.shape[0] // EDGE) * (density.shape[1] // EDGE)
    vmem = pl.BlockSpec(memory_space=pltpu.VMEM)
    return pl.pallas_call(
        functools.partial(send_kernel, outer, inner, row_count),
        out_shape=(
            jax.ShapeDtypeStruct((row_count * col_count, slots, HALF, LANES), jnp.bfloat16),
            jax.ShapeDtypeStruct((up_to(outer, 8), up_to(plane_count * slots, LANES)), jnp.int32),
        ),
        in_specs=[pl.BlockSpec(memory_space=pltpu.SMEM), vmem, vmem],
        out_specs=(pl.BlockSpec(memory_space=pl.ANY), pl.BlockSpec(memory_space=pltpu.SMEM)),
        scratch_shapes=[
            pltpu.VMEM((count + 1, HALF, LANES), jnp.bfloat16),
            pltpu.VMEM((outer, up_to(slots, 8), up_to(devices, LANES)), jnp.int32),
            pltpu.SMEM((outer, up_to(slots, 8), up_to(devices, LANES)), jnp.int32),
            pltpu.VMEM((outer, plane_count, slots, HALF, LANES), jnp.bfloat16),
            pltpu.SemaphoreType.DMA,
            pltpu.SemaphoreType.DMA,
            pltpu.SemaphoreType.DMA,
            pltpu.SemaphoreType.DMA((2, outer)),
            pltpu.SemaphoreType.DMA((2, outer)),
            *LineGather.semaphores(outer, 1),
            *[pltpu.VMEM((count + 1, HALF, LANES), jnp.bfloat16)] * (2 * (outer - 1)),
        ],
        compiler_params=pltpu.CompilerParams(
            vmem_limit_bytes=VMEM_LIMIT, collective_id=1, has_side_effects=True
        ),
        name="send_out",
    )(lists, lists, density)


def back_kernel(
    scale, outer, inner, row_count, kept_ref, mask_ref, slots_ref, core_ref, ham_ref, x0_ref, x3_ref,
    landed, wide, total, sums, arriving, land_sem, send_sem, line_send, line_recv, *rest
):
    plane = Plane(outer, inner, row_count)
    a, b = plane.a, plane.b
    rows, cols = core_ref.shape
    across = cols // EDGE
    count = sums.shape[1]
    slots = slots_ref.shape[1]
    terms = plane.count * slots
    line = LineGather(None, outer, 1, a, plane.on_line, (None,) * 3)
    plane.greet(line)

    def send_plane(target):
        def one(offset, carry):
            place = plane.peer(offset)
            pltpu.make_async_remote_copy(
                src_ref=slots_ref.at[plane.owner(place, target)],
                dst_ref=landed.at[target, plane.place],
                send_sem=send_sem.at[target],
                recv_sem=land_sem.at[target],
                device_id=plane.device(place),
                device_id_type=MESH,
            ).start()
            return carry

        lax.fori_loop(0, plane.count - 1, one, 0)
        pltpu.make_async_copy(
            slots_ref.at[plane.owner(plane.place, target)], landed.at[target, plane.place], land_sem.at[target]
        ).start()

    def combine(target):
        pltpu.make_async_copy(landed.at[target], landed.at[target], land_sem.at[target]).wait()
        wide[...] = landed[target].astype(jnp.float32).reshape(wide.shape)
        numbers = lax.broadcasted_iota(jnp.int32, (count, terms), 0)
        chosen = jnp.where(numbers == kept_ref[pl.ds(target, 1), 0:terms], 1.0, 0.0).astype(jnp.bfloat16)
        for line_at in range(HALF):
            part = wide[pl.ds(line_at, terms, stride=HALF), :].astype(jnp.bfloat16)
            total[pl.ds(line_at, count, stride=HALF), :] = jnp.dot(
                chosen, part, preferred_element_type=jnp.float32
            )

    def wait_line(target, side):
        ref = arriving.at[target, side]
        pltpu.make_async_copy(ref, ref, line_recv.at[target, side]).wait()

    def pass_on(target, step, side):
        return pltpu.make_async_remote_copy(
            src_ref=sums.at[target],
            dst_ref=arriving.at[target, side],
            send_sem=line_send.at[target],
            recv_sem=line_recv.at[target, side],
            device_id=plane.on_line(a + step),
            device_id_type=MESH,
        )

    order = [(d, step) for d in range(outer - 1, 0, -1) for step in (1, -1)] + [(0, 1)]

    def each(d, step, act):
        target = a + d * step

        @pl.when(jnp.logical_and(target >= 0, target < outer))
        def _():
            act(target)

    def nth(k, act):
        far = jnp.maximum(a, outer - 1 - a)
        near = outer - 1 - far
        up = a < outer - 1 - a
        long = far - near
        alone = jnp.where(up, a + far - k, a - far + k)
        rest = k - long
        dist = near - rest // 2
        paired = jnp.where(lax.rem(rest, 2) == 0, a + dist, a - dist)
        act(jnp.where(rest < 0, alone, paired))

    def sent_plane(target):
        sent = landed.at[target, pl.ds(0, plane.count - 1)]
        pltpu.make_async_copy(sent, sent, send_sem.at[target]).wait()

    nth(0, send_plane)
    for k in range(outer):
        nth(k, sent_plane)
        if k + 1 < outer:
            nth(k + 1, send_plane)

        def handle(target):
            combine(target)
            for side, step in ((0, 1), (1, -1)):

                @pl.when((target - a) * step > 0)
                def _():
                    @pl.when(jnp.logical_and(a - step >= 0, a - step < outer))
                    def _():
                        wait_line(target, side)
                        total[...] += arriving[target, side].astype(jnp.float32).reshape(total.shape)

                    sums[target] = total[...].astype(jnp.bfloat16).reshape(sums.shape[1:])
                    pass_on(target, step, side).start()

        nth(k, handle)
    for side, step in ((0, 1), (1, -1)):

        @pl.when(jnp.logical_and(a - step >= 0, a - step < outer))
        def _():
            wait_line(a, side)
            total[...] += arriving[a, side].astype(jnp.float32).reshape(total.shape)

    for i in range(rows // EDGE):
        for j in range(0, across, 2):
            lanes = slice(j * EDGE, (j + 2) * EDGE)
            high, mid, low = i * EDGE, i * EDGE + HALF, (i + 1) * EDGE
            at = (i * across + j) * HALF
            top, bottom = join_pair(total[at : at + HALF, :], total[at + HALF : at + 2 * HALF, :])
            ham_ref[high:mid, lanes] = top
            ham_ref[mid:low, lanes] = bottom
            ks = core_ref[high:low, lanes] + ham_ref[high:low, lanes]
            x0_ref[high:low, lanes] = (block_masks(mask_ref, i, j) * ks * scale).astype(jnp.bfloat16)

    sign_part(plane, mask_ref, x0_ref, x3_ref, *rest)
    for d, step in order:
        if d:
            side = 0 if step > 0 else 1
            each(d, step, lambda target: pass_on(target, step, side).wait_send())


def send_blocks_back(scale, lines, kept, blocks, block_mask, core_ham):
    outer, inner = lines
    row_count, col_count = lax.axis_size("row"), lax.axis_size("col")
    row_lines = (row_count // CORES, CORES)
    plane_count = row_count * inner
    slots = blocks.shape[1]
    rows, cols = core_ham.shape
    count = (rows // EDGE) * (cols // EDGE)
    vmem = pl.BlockSpec(memory_space=pltpu.VMEM)
    return pl.pallas_call(
        functools.partial(back_kernel, scale, outer, inner, row_count),
        out_shape=(
            jax.ShapeDtypeStruct(core_ham.shape, jnp.float32),
            jax.ShapeDtypeStruct(core_ham.shape, jnp.bfloat16),
            jax.ShapeDtypeStruct(core_ham.shape, jnp.float32),
        ),
        in_specs=[vmem, vmem, pl.BlockSpec(memory_space=pl.ANY), vmem],
        out_specs=(vmem,) * 3,
        scratch_shapes=[
            pltpu.VMEM((outer, plane_count, slots, HALF, LANES), jnp.bfloat16),
            pltpu.VMEM((plane_count * slots * HALF, LANES), jnp.float32),
            pltpu.VMEM((count * HALF, LANES), jnp.float32),
            pltpu.VMEM((outer, count, HALF, LANES), jnp.bfloat16),
            pltpu.VMEM((outer, 2, count, HALF, LANES), jnp.bfloat16),
            pltpu.SemaphoreType.DMA((outer,)),
            pltpu.SemaphoreType.DMA((outer,)),
            pltpu.SemaphoreType.DMA((outer,)),
            pltpu.SemaphoreType.DMA((outer, 2)),
            pltpu.VMEM((col_count, rows, cols), jnp.bfloat16),
            pltpu.VMEM((row_count, rows, cols), jnp.bfloat16),
            pltpu.VMEM((row_count, rows, cols), jnp.bfloat16),
            pltpu.VMEM((rows, cols), jnp.float32),
            pltpu.VMEM((rows, cols), jnp.float32),
            *LineGather.semaphores(outer, inner),
            *LineGather.semaphores(inner, outer),
            *LineGather.semaphores(*row_lines),
            *LineGather.semaphores(*row_lines),
        ],
        compiler_params=pltpu.CompilerParams(
            vmem_limit_bytes=VMEM_LIMIT, collective_id=2, has_side_effects=True
        ),
        name="back_and_sign",
    )(kept, block_mask, blocks, core_ham)


def grid_kernel(
    chunk, atoms_ref, recv_ref, basis_hbm, vloc_ref, out_ref, sums, pair_mat, k_all, basis_ref, weighted, sem
):
    cells = basis_ref.shape[1]
    load = pltpu.make_async_copy(basis_hbm, basis_ref, sem)
    load.start()
    sums[...] = jnp.zeros_like(sums)

    owners, slots = recv_ref.shape[:2]

    def pair(owner, slot):
        return atoms_ref[0, slot, owner] * ATOMS + atoms_ref[1, slot, owner]

    def add_slots(owner, carry):
        for slot in range(slots):
            at = pair(owner, slot)
            sums[at] = sums[at] + recv_ref[owner, slot].astype(jnp.float32)
        return carry

    lax.fori_loop(0, owners, add_slots, 0)

    def assemble(a, carry):
        row = pl.multiple_of(a * EDGE, EDGE)
        for b in range(0, ATOMS, 2):
            top, bottom = join_pair(sums[a * ATOMS + b], sums[a * ATOMS + b + 1])
            lanes = slice(b * EDGE, (b + 2) * EDGE)
            pair_mat[pl.ds(row, HALF), lanes] = top.astype(jnp.bfloat16)
            pair_mat[pl.ds(row + HALF, HALF), lanes] = bottom.astype(jnp.bfloat16)
        return carry

    lax.fori_loop(0, ATOMS, assemble, 0)
    columns = 4 * EDGE
    tiles = [slice(start, start + columns) for start in range(0, ATOMS * EDGE, columns)]
    for m, high in enumerate(tiles):
        for low in tiles[m + 1 :]:
            turned = pair_mat[low, high].astype(jnp.float32).T
            pair_mat[high, low] = (pair_mat[high, low].astype(jnp.float32) + turned).astype(jnp.bfloat16)
    load.wait()

    def integrate(step, carry):
        at = pl.ds(pl.multiple_of(step * chunk, chunk), chunk)
        rho = jnp.zeros((1, chunk), jnp.float32)
        for high in tiles:
            mixed = jnp.dot(
                pair_mat[high, high.start :], basis_ref[high.start :, at], preferred_element_type=jnp.float32
            )
            rho += jnp.sum(basis_ref[high, at].astype(jnp.float32) * mixed, axis=0, keepdims=True)
        wide = basis_ref[:, at].astype(jnp.float32)
        pot = vloc_ref[:, at] + 0.5 * rho / jnp.sqrt(1.0 + rho * rho)
        weighted[:, at] = (wide * pot).astype(jnp.bfloat16)
        return carry

    lax.fori_loop(0, cells // chunk, integrate, 0)
    for n, low in enumerate(tiles):
        k_all[: low.stop, low] = lax.dot_general(
            weighted[: low.stop, :], basis_ref[low, :], (((1,), (1,)), ((), ())), preferred_element_type=jnp.float32
        )
        for high in tiles[:n]:
            k_all[low, high] = k_all[high, low].T

    def split(a, carry):
        row = pl.multiple_of(a * EDGE, EDGE)
        for b in range(0, ATOMS, 2):
            lanes = slice(b * EDGE, (b + 2) * EDGE)
            first, second = split_pair(k_all[pl.ds(row, HALF), lanes], k_all[pl.ds(row + HALF, HALF), lanes])
            sums[a * ATOMS + b] = first
            sums[a * ATOMS + b + 1] = second
        return carry

    lax.fori_loop(0, ATOMS, split, 0)

    def give_slots(owner, carry):
        for slot in range(slots):
            out_ref[owner, slot] = sums[pair(owner, slot)].astype(jnp.bfloat16)
        return carry

    lax.fori_loop(0, owners, give_slots, 0)


def grid_step(atoms, received, basis, v_loc):
    order = ATOMS * EDGE
    chunk = math.gcd(basis.shape[1], 512)
    return pl.pallas_call(
        functools.partial(grid_kernel, chunk),
        out_shape=jax.ShapeDtypeStruct(received.shape, jnp.bfloat16),
        in_specs=[
            pl.BlockSpec(memory_space=pltpu.SMEM),
            pl.BlockSpec(memory_space=pltpu.VMEM),
            pl.BlockSpec(memory_space=pl.ANY),
            pl.BlockSpec(memory_space=pltpu.VMEM),
        ],
        out_specs=pl.BlockSpec(memory_space=pltpu.VMEM),
        scratch_shapes=[
            pltpu.VMEM((ATOMS * ATOMS, HALF, LANES), jnp.float32),
            pltpu.VMEM((order, order), jnp.bfloat16),
            pltpu.VMEM((order, order), jnp.float32),
            pltpu.VMEM(basis.shape, jnp.bfloat16),
            pltpu.VMEM(basis.shape, jnp.bfloat16),
            pltpu.SemaphoreType.DMA,
        ],
        compiler_params=pltpu.CompilerParams(vmem_limit_bytes=VMEM_LIMIT),
        name="grid",
    )(atoms, received, basis, v_loc)


def block_masks(mask_ref, i, j):
    low = lax.broadcasted_iota(jnp.int32, (EDGE, LANES), 1) < EDGE
    left, right = mask_ref[j : j + 1, i : i + 1], mask_ref[j + 1 : j + 2, i : i + 1]
    return jnp.where(low, left.astype(jnp.float32), right.astype(jnp.float32))


class LineGather:
    def __init__(self, piece, outer, inner, place, device_at, sems):
        self.piece, self.outer, self.inner = piece, outer, inner
        self.a, self.b = place // inner, place % inner
        self.device_at = device_at
        self.out_sem, self.in_sem, self.recv_sem = sems
        self.sent = []

    def neighbours(self):
        a, b = self.a, self.b
        return (
            (a > 0, a - 1, b),
            (a < self.outer - 1, a + 1, b),
            (b > 0, a, b - 1),
            (b < self.inner - 1, a, b + 1),
        )

    def send(self, cond, source, target, sem):
        def describe():
            return pltpu.make_async_remote_copy(
                src_ref=self.piece(source),
                dst_ref=self.piece(source),
                send_sem=sem,
                recv_sem=self.recv_sem.at[source],
                device_id=self.device_at(target),
                device_id_type=MESH,
            )

        @pl.when(cond)
        def _():
            describe().start()

        self.sent.append((cond, describe))

    def arrive(self, source):
        pltpu.make_async_copy(self.piece(source), self.piece(source), self.recv_sem.at[source]).wait()

    def along_inner(self, cond, outer_at, inner_from, step, sem):
        target = self.b + step
        fits = jnp.logical_and(target >= 0, target < self.inner)
        self.send(
            jnp.logical_and(cond, fits), outer_at * self.inner + inner_from, self.a * self.inner + target, sem
        )

    def begin(self):
        self.going = self.steps()
        next(self.going)

    def steps(self):
        a, b, inner = self.a, self.b, self.inner
        for d in range(self.outer):
            for way, step in enumerate((1, -1)):
                if d == 0 and way == 1:
                    have = a >= 0
                    source = a
                else:
                    source = a - d * step
                    have = jnp.logical_and(source >= 0, source < self.outer)
                tile = source * inner + b
                if d > 0:

                    @pl.when(have)
                    def _():
                        self.arrive(tile)

                target = a + step
                fits = jnp.logical_and(target >= 0, target < self.outer)
                self.send(jnp.logical_and(have, fits), tile, target * inner + b, self.out_sem.at[d, way])
                if d > 0 or way == 0:
                    for side, hop in enumerate((1, -1)):
                        self.along_inner(have, source, b, hop, self.in_sem.at[d * 2 + way, side])
            yield
        used = 2 * self.outer
        for e in range(1, inner):
            for outer_at in range(self.outer):
                for way, step in enumerate((1, -1)):
                    origin = b - e * step
                    have = jnp.logical_and(origin >= 0, origin < inner)
                    tile = outer_at * inner + origin

                    @pl.when(have)
                    def _():
                        self.arrive(tile)

                    if e < inner - 1:
                        self.along_inner(have, outer_at, origin, step, self.in_sem.at[used, way])
                if e < inner - 1:
                    used += 1
            yield

    def drain(self):
        for cond, describe in self.sent:

            @pl.when(cond)
            def _():
                describe().wait_send()

    @staticmethod
    def semaphores(outer, inner):
        return [
            pltpu.SemaphoreType.DMA((outer, 2)),
            pltpu.SemaphoreType.DMA((2 * outer + max(inner - 2, 0) * outer, 2)),
            pltpu.SemaphoreType.DMA((outer * inner,)),
        ]


def greet(gathers, others=0):
    barrier = pltpu.get_barrier_semaphore()
    count = others
    for gather in gathers:
        for cond, a, b in gather.neighbours():

            @pl.when(cond)
            def _():
                pl.semaphore_signal(
                    barrier, inc=1, device_id=gather.device_at(a * gather.inner + b), device_id_type=MESH
                )

            count = count + cond.astype(jnp.int32)
    pl.semaphore_wait(barrier, count)


def run_together(*gathers):
    going = [gather.going for gather in gathers]
    while going:
        going = [steps for steps in going if next(steps, "end") is None]


def add_product(acc, left, right, place):
    width = left.shape[2]
    share = right.shape[1] // width
    for part in range(share):
        piece = right[place, part * width : (part + 1) * width, :]
        acc[...] += jnp.dot(left[place * share + part], piece, preferred_element_type=jnp.float32)


def first_rows(rows, outer, inner):
    if inner == 1 or outer == 1:
        return rows
    share = ((outer - 1) * inner - (inner - 1)) / (2 * (outer - 1) * (inner - 1))
    return min(rows - 16, max(16, round(share * rows / 16) * 16))


def sign_part(plane, mask_ref, x0_ref, x3_ref, left, right, second, mask, acc, *sems):
    row, outer, inner = plane.row, plane.outer, plane.inner
    col = plane.a * inner + plane.b
    rows, cols = x0_ref.shape
    row_lines = (right.shape[0] // CORES, CORES)
    split = first_rows(rows, outer, inner)

    def turned(at):
        return (at % outer) * inner + at // outer

    gathers = [
        LineGather(
            lambda at: left.at[at, pl.ds(0, split)], outer, inner, col, lambda at: (row, at), sems[0:3]
        ),
        LineGather(right.at.__getitem__, *row_lines, row, lambda at: (at, col), sems[6:9]),
    ]
    if split < rows:
        gathers.insert(
            1,
            LineGather(
                lambda at: left.at[turned(at), pl.ds(split, rows - split)],
                inner,
                outer,
                plane.b * outer + plane.a,
                lambda at: (row, turned(at)),
                sems[3:6],
            ),
        )
    again = LineGather(second.at.__getitem__, *row_lines, row, lambda at: (at, col), sems[9:12])
    left[col] = x0_ref[...]
    right[row] = x0_ref[...]
    for gather in gathers:
        gather.begin()
    for i in range(rows // EDGE):
        for j in range(0, cols // EDGE, 2):
            mask[i * EDGE : (i + 1) * EDGE, j * EDGE : (j + 2) * EDGE] = block_masks(mask_ref, i, j)
    run_together(*gathers)
    acc[...] = jnp.zeros_like(acc)
    for place in range(right.shape[0]):
        add_product(acc, left, right, place)
    second[row] = (mask[...] * acc[...]).astype(jnp.bfloat16)
    again.begin()
    acc[...] = jnp.zeros_like(acc)
    add_product(acc, left, second, row)
    run_together(again)
    for offset in range(1, right.shape[0]):
        add_product(acc, left, second, lax.rem(row + offset, right.shape[0]))
    x3_ref[...] = mask[...] * acc[...]
    for gather in (*gathers, again):
        gather.drain()


def finish_kernel(scale, core_ref, ham_ref, x0_ref, x3_ref, ks_ref, sign_ref):
    ks_ref[...] = core_ref[...] + ham_ref[...]
    sign_ref[...] = (1.5 * x0_ref[...].astype(jnp.float32) - 0.5 * x3_ref[...]) / scale


def finish(scale, core_ham, ham_tile, x0, x3):
    rows, cols = core_ham.shape
    share = pl.BlockSpec((rows // 2, cols), lambda i: (i, 0))
    return pl.pallas_call(
        functools.partial(finish_kernel, scale),
        out_shape=(jax.ShapeDtypeStruct(core_ham.shape, jnp.float32),) * 2,
        grid=(2,),
        in_specs=[share] * 4,
        out_specs=(share,) * 2,
        compiler_params=pltpu.CompilerParams(vmem_limit_bytes=VMEM_LIMIT),
        name="finish",
    )(core_ham, ham_tile, x0, x3)


def body(density, core_ham, block_mask, send_blocks, task_atoms, basis, v_loc):
    row_count, col_count = lax.axis_size("row"), lax.axis_size("col")
    block_rows = density.shape[0] // EDGE
    outer = math.gcd(col_count, 4)
    inner = col_count // outer
    received, kept = send_blocks_out((outer, inner), send_blocks[0].T, density)
    k_slot = grid_step(task_atoms[:, 0].transpose(0, 2, 1), received, basis[0], v_loc)
    scale = 1.0 / math.sqrt(16.0 * block_rows * row_count)
    parts = send_blocks_back(scale, (outer, inner), kept, k_slot, block_mask.T, core_ham)
    return finish(scale, core_ham, *parts)


def solution(mesh):
    placed = (
        P("row", "col"),
        P("row", "col"),
        P("row", "col"),
        P(("row", "col"), None, None),
        P(None, ("row", "col"), None, None),
        P(("row", "col"), None, None),
        P(("row", "col"), None),
    )
    return jax.shard_map(
        body,
        mesh=mesh,
        in_specs=placed,
        out_specs=(P("row", "col"), P("row", "col")),
        check_vma=False,
    )
```

```python
import functools
import math

import jax
import jax.numpy as jnp
from jax import lax
from jax.experimental import pallas as pl
from jax.experimental.pallas import tpu as pltpu
from jax.sharding import PartitionSpec as P

ATOMS = 16
EDGE = 64
HALF = EDGE // 2
LANES = 2 * EDGE
CORES = 2
CHUNKS = 4
MESH = pl.DeviceIdType.MESH
VMEM_LIMIT = 56 * 1024 * 1024


def low_lanes():
    return lax.broadcasted_iota(jnp.int32, (HALF, LANES), 1) < EDGE


def join_pair(first, second):
    low = low_lanes()
    top = jnp.where(low, first, pltpu.roll(second, EDGE, 1))
    bottom = jnp.where(low, pltpu.roll(first, EDGE, 1), second)
    return top, bottom


def split_pair(top, bottom):
    return join_pair(top, bottom)


class Plane:
    def __init__(self, outer, inner, row_count):
        self.outer, self.inner, self.count = outer, inner, row_count * inner
        self.row, col = lax.axis_index("row"), lax.axis_index("col")
        self.a, self.b = col // inner, col % inner
        self.place = self.row * inner + self.b

    def peer(self, offset):
        return lax.rem(self.place + 1 + offset, self.count)

    def device(self, place):
        return (place // self.inner, self.a * self.inner + place % self.inner)

    def owner(self, place, outer_at):
        return (place // self.inner) * (self.outer * self.inner) + outer_at * self.inner + place % self.inner

    def on_line(self, outer_at):
        return (self.row, outer_at * self.inner + self.b)

    def greet(self, line):
        barrier = pltpu.get_barrier_semaphore()

        def signal(offset, carry):
            pl.semaphore_signal(barrier, inc=1, device_id=self.device(self.peer(offset)), device_id_type=MESH)
            return carry

        lax.fori_loop(0, self.count - 1, signal, 0)
        greet([line], self.count - 1)


def send_kernel(
    outer, inner, row_count, index_ref, lists_ref, density_ref, out_ref, kept_ref,
    own, lists, lists_smem, stage, list_sem, recv_sem, send_sem, tile_send, tile_recv, *rest
):
    plane = Plane(outer, inner, row_count)
    a = plane.a
    rows, cols = density_ref.shape
    across = cols // EDGE
    count = (rows // EDGE) * across
    slots = stage.shape[2]
    entries = LineGather(lists.at.__getitem__, outer, 1, a, plane.on_line, rest[0:3])
    arrived = (rest[3 : 2 + outer], rest[2 + outer :])
    for tile in (own, *arrived[0], *arrived[1]):
        tile[count] = jnp.zeros((HALF, LANES), tile.dtype)
    lists[a] = jnp.zeros(lists.shape[1:], jnp.int32)
    lists[a, 0 : lists_ref.shape[0], 0 : lists_ref.shape[1]] = lists_ref[...]
    for i in range(rows // EDGE):
        for j in range(0, across, 2):
            lanes = slice(j * EDGE, (j + 2) * EDGE)
            top = density_ref[i * EDGE : i * EDGE + HALF, lanes].astype(jnp.float32)
            bottom = density_ref[i * EDGE + HALF : (i + 1) * EDGE, lanes].astype(jnp.float32)
            first, second = split_pair(top, bottom)
            own[i * across + j] = first.astype(own.dtype)
            own[i * across + j + 1] = second.astype(own.dtype)
    plane.greet(entries)

    def passes(d, step):
        source, target = a - d * step, a + step
        return jnp.logical_and(
            jnp.logical_and(source >= 0, source < outer), jnp.logical_and(target >= 0, target < outer)
        )

    def pass_on(d, way, step):
        tile = arrived[way][d - 1] if d else own
        return pltpu.make_async_remote_copy(
            src_ref=tile.at[pl.ds(0, count)],
            dst_ref=arrived[way][d].at[pl.ds(0, count)],
            send_sem=tile_send.at[way, d],
            recv_sem=tile_recv.at[way, d],
            device_id=plane.on_line(a + step),
            device_id_type=MESH,
        )

    def serve(tile, source, number):
        def pick(offset, place):
            target = plane.owner(place, a)
            for slot in range(slots):
                found = number(slot, target)
                local = jnp.where(found >= 0, found, count)
                stage[source, offset, slot] = tile[local]
                kept_ref[source, place * slots + slot] = local

        def one(offset, carry):
            place = plane.peer(offset)
            pick(offset, place)
            pltpu.make_async_remote_copy(
                src_ref=stage.at[source, offset],
                dst_ref=out_ref.at[plane.owner(plane.place, source)],
                send_sem=send_sem,
                recv_sem=recv_sem,
                device_id=plane.device(place),
                device_id_type=MESH,
            ).start()
            return carry

        lax.fori_loop(0, plane.count - 1, one, 0)
        pick(plane.count - 1, plane.place)
        pltpu.make_async_copy(
            stage.at[source, plane.count - 1], out_ref.at[plane.owner(plane.place, source)], recv_sem
        ).start()

    entry_steps = entries.steps()
    for d in range(outer):
        next(entry_steps, None)
        if d:
            for way, step in enumerate((1, -1)):
                source = a - d * step

                @pl.when(jnp.logical_and(source >= 0, source < outer))
                def _():
                    copy = pltpu.make_async_copy(lists.at[source], lists_smem.at[source], list_sem)
                    copy.start()
                    copy.wait()
                    tile = arrived[way][d - 1].at[pl.ds(0, count)]
                    pltpu.make_async_copy(tile, tile, tile_recv.at[way, d - 1]).wait()

        if d < outer - 1:
            for way, step in enumerate((1, -1)):

                @pl.when(passes(d, step))
                def _():
                    pass_on(d, way, step).start()

        if d == 0:
            serve(own, a, lambda slot, at: index_ref[slot, at])
            continue
        for way, step in enumerate((1, -1)):
            source = a - d * step

            @pl.when(jnp.logical_and(source >= 0, source < outer))
            def _():
                serve(arrived[way][d - 1], source, lambda slot, at: lists_smem[source, slot, at])

    for d in range(outer - 1):
        for way, step in enumerate((1, -1)):

            @pl.when(passes(d, step))
            def _():
                pass_on(d, way, step).wait_send()

    entries.drain()
    sent = stage.at[:, pl.ds(0, plane.count - 1)]
    pltpu.make_async_copy(sent, sent, send_sem).wait()
    pltpu.make_async_copy(out_ref, out_ref, recv_sem).wait()


def up_to(size, step):
    return size + -size % step


def send_blocks_out(lines, lists, density):
    outer, inner = lines
    slots, devices = lists.shape
    row_count, col_count = lax.axis_size("row"), lax.axis_size("col")
    plane_count = row_count * inner
    count = (density.shape[0] // EDGE) * (density.shape[1] // EDGE)
    vmem = pl.BlockSpec(memory_space=pltpu.VMEM)
    return pl.pallas_call(
        functools.partial(send_kernel, outer, inner, row_count),
        out_shape=(
            jax.ShapeDtypeStruct((row_count * col_count, slots, HALF, LANES), jnp.bfloat16),
            jax.ShapeDtypeStruct((up_to(outer, 8), up_to(plane_count * slots, LANES)), jnp.int32),
        ),
        in_specs=[pl.BlockSpec(memory_space=pltpu.SMEM), vmem, vmem],
        out_specs=(pl.BlockSpec(memory_space=pl.ANY), pl.BlockSpec(memory_space=pltpu.SMEM)),
        scratch_shapes=[
            pltpu.VMEM((count + 1, HALF, LANES), jnp.bfloat16),
            pltpu.VMEM((outer, up_to(slots, 8), up_to(devices, LANES)), jnp.int32),
            pltpu.SMEM((outer, up_to(slots, 8), up_to(devices, LANES)), jnp.int32),
            pltpu.VMEM((outer, plane_count, slots, HALF, LANES), jnp.bfloat16),
            pltpu.SemaphoreType.DMA,
            pltpu.SemaphoreType.DMA,
            pltpu.SemaphoreType.DMA,
            pltpu.SemaphoreType.DMA((2, outer)),
            pltpu.SemaphoreType.DMA((2, outer)),
            *LineGather.semaphores(outer, 1),
            *[pltpu.VMEM((count + 1, HALF, LANES), jnp.bfloat16)] * (2 * (outer - 1)),
        ],
        compiler_params=pltpu.CompilerParams(
            vmem_limit_bytes=VMEM_LIMIT, collective_id=1, has_side_effects=True
        ),
        name="send_out",
    )(lists, lists, density)


def back_kernel(
    scale, outer, inner, row_count, kept_ref, mask_ref, slots_ref, core_ref, ham_ref, x0_ref, x3_ref,
    landed, wide, first_total, second_total, sums, arriving, land_sem, send_sem, line_send, line_recv, *rest
):
    plane = Plane(outer, inner, row_count)
    a, b = plane.a, plane.b
    rows, cols = core_ref.shape
    across = cols // EDGE
    count = sums.shape[1]
    slots = slots_ref.shape[1]
    terms = plane.count * slots
    line = LineGather(None, outer, 1, a, plane.on_line, (None,) * 3)
    plane.greet(line)

    def send_plane(target):
        def one(offset, carry):
            place = plane.peer(offset)
            pltpu.make_async_remote_copy(
                src_ref=slots_ref.at[plane.owner(place, target)],
                dst_ref=landed.at[target, plane.place],
                send_sem=send_sem.at[target],
                recv_sem=land_sem.at[target],
                device_id=plane.device(place),
                device_id_type=MESH,
            ).start()
            return carry

        lax.fori_loop(0, plane.count - 1, one, 0)
        pltpu.make_async_copy(
            slots_ref.at[plane.owner(plane.place, target)], landed.at[target, plane.place], land_sem.at[target]
        ).start()

    def combine(target, total):
        pltpu.make_async_copy(landed.at[target], landed.at[target], land_sem.at[target]).wait()
        wide[...] = landed[target].astype(jnp.float32).reshape(wide.shape)
        numbers = lax.broadcasted_iota(jnp.int32, (count, terms), 0)
        chosen = jnp.where(numbers == kept_ref[pl.ds(target, 1), 0:terms], 1.0, 0.0).astype(jnp.bfloat16)
        for line_at in range(HALF):
            part = wide[pl.ds(line_at, terms, stride=HALF), :].astype(jnp.bfloat16)
            total[pl.ds(line_at, count, stride=HALF), :] = jnp.dot(
                chosen, part, preferred_element_type=jnp.float32
            )

    def wait_line(target, side):
        ref = arriving.at[target, side]
        pltpu.make_async_copy(ref, ref, line_recv.at[target, side]).wait()

    def pass_on(target, step, side):
        return pltpu.make_async_remote_copy(
            src_ref=sums.at[target],
            dst_ref=arriving.at[target, side],
            send_sem=line_send.at[target],
            recv_sem=line_recv.at[target, side],
            device_id=plane.on_line(a + step),
            device_id_type=MESH,
        )

    order = [(d, step) for d in range(outer - 1, 0, -1) for step in (1, -1)] + [(0, 1)]

    def each(d, step, act):
        target = a + d * step

        @pl.when(jnp.logical_and(target >= 0, target < outer))
        def _():
            act(target)

    def nth(k, act):
        far = jnp.maximum(a, outer - 1 - a)
        near = outer - 1 - far
        up = a < outer - 1 - a
        long = far - near
        alone = jnp.where(up, a + far - k, a - far + k)
        rest = k - long
        dist = near - rest // 2
        paired = jnp.where(lax.rem(rest, 2) == 0, a + dist, a - dist)
        act(jnp.where(rest < 0, alone, paired))

    def sent_plane(target):
        sent = landed.at[target, pl.ds(0, plane.count - 1)]
        pltpu.make_async_copy(sent, sent, send_sem.at[target]).wait()

    nth(0, send_plane)
    totals = (first_total, second_total)

    def pass_total(k, with_line):
        total = totals[k % 2]

        def handle(target):
            for side, step in ((0, 1), (1, -1)):
                inside = jnp.logical_and(a - step >= 0, a - step < outer)
                fits = inside if with_line else jnp.logical_not(inside)

                @pl.when(jnp.logical_and((target - a) * step > 0, fits))
                def _():
                    if with_line:
                        wait_line(target, side)
                        total[...] += arriving[target, side].astype(jnp.float32).reshape(total.shape)
                    sums[target] = total[...].astype(jnp.bfloat16).reshape(sums.shape[1:])
                    pass_on(target, step, side).start()

        nth(k, handle)

    for k in range(outer):
        nth(k, sent_plane)
        if k + 1 < outer:
            nth(k + 1, send_plane)
        nth(k, lambda target: combine(target, totals[k % 2]))
        pass_total(k, False)
        if k:
            pass_total(k - 1, True)
    total = totals[(outer - 1) % 2]
    for side, step in ((0, 1), (1, -1)):

        @pl.when(jnp.logical_and(a - step >= 0, a - step < outer))
        def _():
            wait_line(a, side)
            total[...] += arriving[a, side].astype(jnp.float32).reshape(total.shape)

    for i in range(rows // EDGE):
        for j in range(0, across, 2):
            lanes = slice(j * EDGE, (j + 2) * EDGE)
            high, mid, low = i * EDGE, i * EDGE + HALF, (i + 1) * EDGE
            at = (i * across + j) * HALF
            top, bottom = join_pair(total[at : at + HALF, :], total[at + HALF : at + 2 * HALF, :])
            ham_ref[high:mid, lanes] = top
            ham_ref[mid:low, lanes] = bottom
            ks = core_ref[high:low, lanes] + ham_ref[high:low, lanes]
            x0_ref[high:low, lanes] = (block_masks(mask_ref, i, j) * ks * scale).astype(jnp.bfloat16)

    sign_part(plane, mask_ref, x0_ref, x3_ref, *rest)
    for d, step in order:
        if d:
            side = 0 if step > 0 else 1
            each(d, step, lambda target: pass_on(target, step, side).wait_send())


def send_blocks_back(scale, lines, kept, blocks, block_mask, core_ham):
    outer, inner = lines
    row_count, col_count = lax.axis_size("row"), lax.axis_size("col")
    row_lines = (row_count // CORES, CORES)
    plane_count = row_count * inner
    slots = blocks.shape[1]
    rows, cols = core_ham.shape
    count = (rows // EDGE) * (cols // EDGE)
    vmem = pl.BlockSpec(memory_space=pltpu.VMEM)
    return pl.pallas_call(
        functools.partial(back_kernel, scale, outer, inner, row_count),
        out_shape=(
            jax.ShapeDtypeStruct(core_ham.shape, jnp.float32),
            jax.ShapeDtypeStruct(core_ham.shape, jnp.bfloat16),
            jax.ShapeDtypeStruct(core_ham.shape, jnp.float32),
        ),
        in_specs=[vmem, vmem, pl.BlockSpec(memory_space=pl.ANY), vmem],
        out_specs=(vmem,) * 3,
        scratch_shapes=[
            pltpu.VMEM((outer, plane_count, slots, HALF, LANES), jnp.bfloat16),
            pltpu.VMEM((plane_count * slots * HALF, LANES), jnp.float32),
            pltpu.VMEM((count * HALF, LANES), jnp.float32),
            pltpu.VMEM((count * HALF, LANES), jnp.float32),
            pltpu.VMEM((outer, count, HALF, LANES), jnp.bfloat16),
            pltpu.VMEM((outer, 2, count, HALF, LANES), jnp.bfloat16),
            pltpu.SemaphoreType.DMA((outer,)),
            pltpu.SemaphoreType.DMA((outer,)),
            pltpu.SemaphoreType.DMA((outer,)),
            pltpu.SemaphoreType.DMA((outer, 2)),
            pltpu.VMEM((col_count, rows, cols), jnp.bfloat16),
            pltpu.VMEM((row_count, rows, cols), jnp.bfloat16),
            pltpu.VMEM((row_count, rows, cols), jnp.bfloat16),
            pltpu.VMEM((rows, cols), jnp.float32),
            pltpu.VMEM((rows, cols), jnp.float32),
            *LineGather.semaphores(*row_lines),
            *[
                sem
                for turned in turned_chunks(outer, inner)
                for sem in LineGather.semaphores(*((inner, outer) if turned else (outer, inner)))
            ],
            *LineGather.semaphores(*row_lines) * CHUNKS,
        ],
        compiler_params=pltpu.CompilerParams(
            vmem_limit_bytes=VMEM_LIMIT, collective_id=2, has_side_effects=True
        ),
        name="back_and_sign",
    )(kept, block_mask, blocks, core_ham)


def grid_kernel(
    chunk, atoms_ref, recv_ref, basis_hbm, vloc_ref, out_ref, sums, pair_mat, k_all, basis_ref, weighted, sem
):
    cells = basis_ref.shape[1]
    load = pltpu.make_async_copy(basis_hbm, basis_ref, sem)
    load.start()
    sums[...] = jnp.zeros_like(sums)

    owners, slots = recv_ref.shape[:2]

    def pair(owner, slot):
        return atoms_ref[0, slot, owner] * ATOMS + atoms_ref[1, slot, owner]

    def add_slots(owner, carry):
        for slot in range(slots):
            at = pair(owner, slot)
            sums[at] = sums[at] + recv_ref[owner, slot].astype(jnp.float32)
        return carry

    lax.fori_loop(0, owners, add_slots, 0)

    def assemble(a, carry):
        row = pl.multiple_of(a * EDGE, EDGE)
        for b in range(0, ATOMS, 2):
            top, bottom = join_pair(sums[a * ATOMS + b], sums[a * ATOMS + b + 1])
            lanes = slice(b * EDGE, (b + 2) * EDGE)
            pair_mat[pl.ds(row, HALF), lanes] = top.astype(jnp.bfloat16)
            pair_mat[pl.ds(row + HALF, HALF), lanes] = bottom.astype(jnp.bfloat16)
        return carry

    lax.fori_loop(0, ATOMS, assemble, 0)
    columns = 4 * EDGE
    tiles = [slice(start, start + columns) for start in range(0, ATOMS * EDGE, columns)]
    for m, high in enumerate(tiles):
        for low in tiles[m + 1 :]:
            turned = pair_mat[low, high].astype(jnp.float32).T
            pair_mat[high, low] = (pair_mat[high, low].astype(jnp.float32) + turned).astype(jnp.bfloat16)
    load.wait()

    def integrate(step, carry):
        at = pl.ds(pl.multiple_of(step * chunk, chunk), chunk)
        rho = jnp.zeros((1, chunk), jnp.float32)
        for high in tiles:
            mixed = jnp.dot(
                pair_mat[high, high.start :], basis_ref[high.start :, at], preferred_element_type=jnp.float32
            )
            rho += jnp.sum(basis_ref[high, at].astype(jnp.float32) * mixed, axis=0, keepdims=True)
        wide = basis_ref[:, at].astype(jnp.float32)
        pot = vloc_ref[:, at] + 0.5 * rho / jnp.sqrt(1.0 + rho * rho)
        weighted[:, at] = (wide * pot).astype(jnp.bfloat16)
        return carry

    lax.fori_loop(0, cells // chunk, integrate, 0)
    for n, low in enumerate(tiles):
        k_all[: low.stop, low] = lax.dot_general(
            weighted[: low.stop, :], basis_ref[low, :], (((1,), (1,)), ((), ())), preferred_element_type=jnp.float32
        )
        for high in tiles[:n]:
            k_all[low, high] = k_all[high, low].T

    def split(a, carry):
        row = pl.multiple_of(a * EDGE, EDGE)
        for b in range(0, ATOMS, 2):
            lanes = slice(b * EDGE, (b + 2) * EDGE)
            first, second = split_pair(k_all[pl.ds(row, HALF), lanes], k_all[pl.ds(row + HALF, HALF), lanes])
            sums[a * ATOMS + b] = first
            sums[a * ATOMS + b + 1] = second
        return carry

    lax.fori_loop(0, ATOMS, split, 0)

    def give_slots(owner, carry):
        for slot in range(slots):
            out_ref[owner, slot] = sums[pair(owner, slot)].astype(jnp.bfloat16)
        return carry

    lax.fori_loop(0, owners, give_slots, 0)


def grid_step(atoms, received, basis, v_loc):
    order = ATOMS * EDGE
    chunk = math.gcd(basis.shape[1], 512)
    return pl.pallas_call(
        functools.partial(grid_kernel, chunk),
        out_shape=jax.ShapeDtypeStruct(received.shape, jnp.bfloat16),
        in_specs=[
            pl.BlockSpec(memory_space=pltpu.SMEM),
            pl.BlockSpec(memory_space=pltpu.VMEM),
            pl.BlockSpec(memory_space=pl.ANY),
            pl.BlockSpec(memory_space=pltpu.VMEM),
        ],
        out_specs=pl.BlockSpec(memory_space=pltpu.VMEM),
        scratch_shapes=[
            pltpu.VMEM((ATOMS * ATOMS, HALF, LANES), jnp.float32),
            pltpu.VMEM((order, order), jnp.bfloat16),
            pltpu.VMEM((order, order), jnp.float32),
            pltpu.VMEM(basis.shape, jnp.bfloat16),
            pltpu.VMEM(basis.shape, jnp.bfloat16),
            pltpu.SemaphoreType.DMA,
        ],
        compiler_params=pltpu.CompilerParams(vmem_limit_bytes=VMEM_LIMIT),
        name="grid",
    )(atoms, received, basis, v_loc)


def block_masks(mask_ref, i, j):
    low = lax.broadcasted_iota(jnp.int32, (EDGE, LANES), 1) < EDGE
    left, right = mask_ref[j : j + 1, i : i + 1], mask_ref[j + 1 : j + 2, i : i + 1]
    return jnp.where(low, left.astype(jnp.float32), right.astype(jnp.float32))


class LineGather:
    def __init__(self, piece, outer, inner, place, device_at, sems):
        self.piece, self.outer, self.inner = piece, outer, inner
        self.a, self.b = place // inner, place % inner
        self.device_at = device_at
        self.out_sem, self.in_sem, self.recv_sem = sems
        self.sent = []

    def neighbours(self):
        a, b = self.a, self.b
        return (
            (a > 0, a - 1, b),
            (a < self.outer - 1, a + 1, b),
            (b > 0, a, b - 1),
            (b < self.inner - 1, a, b + 1),
        )

    def send(self, cond, source, target, sem):
        def describe():
            return pltpu.make_async_remote_copy(
                src_ref=self.piece(source),
                dst_ref=self.piece(source),
                send_sem=sem,
                recv_sem=self.recv_sem.at[source],
                device_id=self.device_at(target),
                device_id_type=MESH,
            )

        @pl.when(cond)
        def _():
            describe().start()

        self.sent.append((cond, describe))

    def arrive(self, source):
        pltpu.make_async_copy(self.piece(source), self.piece(source), self.recv_sem.at[source]).wait()

    def along_inner(self, cond, outer_at, inner_from, step, sem):
        target = self.b + step
        fits = jnp.logical_and(target >= 0, target < self.inner)
        self.send(
            jnp.logical_and(cond, fits), outer_at * self.inner + inner_from, self.a * self.inner + target, sem
        )

    def begin(self):
        self.going = self.steps()
        next(self.going, None)

    def steps(self):
        a, b, inner = self.a, self.b, self.inner
        for d in range(self.outer):
            for way, step in enumerate((1, -1)):
                if d == 0 and way == 1:
                    have = a >= 0
                    source = a
                else:
                    source = a - d * step
                    have = jnp.logical_and(source >= 0, source < self.outer)
                tile = source * inner + b
                if d > 0:

                    @pl.when(have)
                    def _():
                        self.arrive(tile)

                target = a + step
                fits = jnp.logical_and(target >= 0, target < self.outer)
                self.send(jnp.logical_and(have, fits), tile, target * inner + b, self.out_sem.at[d, way])
                if d > 0 or way == 0:
                    for side, hop in enumerate((1, -1)):
                        self.along_inner(have, source, b, hop, self.in_sem.at[d * 2 + way, side])
            if inner > 1 or d < self.outer - 1:
                yield
        used = 2 * self.outer
        for e in range(1, inner):
            for outer_at in range(self.outer):
                for way, step in enumerate((1, -1)):
                    origin = b - e * step
                    have = jnp.logical_and(origin >= 0, origin < inner)
                    tile = outer_at * inner + origin

                    @pl.when(have)
                    def _():
                        self.arrive(tile)

                    if e < inner - 1:
                        self.along_inner(have, outer_at, origin, step, self.in_sem.at[used, way])
                if e < inner - 1:
                    used += 1
            if e < inner - 1:
                yield

    def drain(self):
        for cond, describe in self.sent:

            @pl.when(cond)
            def _():
                describe().wait_send()

    @staticmethod
    def semaphores(outer, inner):
        return [
            pltpu.SemaphoreType.DMA((outer, 2)),
            pltpu.SemaphoreType.DMA((2 * outer + max(inner - 2, 0) * outer, 2)),
            pltpu.SemaphoreType.DMA((outer * inner,)),
        ]


def greet(gathers, others=0):
    barrier = pltpu.get_barrier_semaphore()
    count = others
    for gather in gathers:
        for cond, a, b in gather.neighbours():

            @pl.when(cond)
            def _():
                pl.semaphore_signal(
                    barrier, inc=1, device_id=gather.device_at(a * gather.inner + b), device_id_type=MESH
                )

            count = count + cond.astype(jnp.int32)
    pl.semaphore_wait(barrier, count)


def add_product(acc, left, right, place, rows=slice(None)):
    width = left.shape[2]
    share = right.shape[1] // width
    for part in range(share):
        piece = right[place, part * width : (part + 1) * width, :]
        acc[rows, :] += jnp.dot(left[place * share + part, rows, :], piece, preferred_element_type=jnp.float32)


def turned_chunks(outer, inner):
    if inner == 1 or outer == 1:
        return (False,) * CHUNKS
    share = ((outer - 1) * inner - (inner - 1)) / (2 * (outer - 1) * (inner - 1))
    straight = min(CHUNKS, max(0, round(share * CHUNKS)))
    return (False,) * straight + (True,) * (CHUNKS - straight)


def sign_part(plane, mask_ref, x0_ref, x3_ref, left, right, second, mask, acc, *sems):
    row, outer, inner = plane.row, plane.outer, plane.inner
    col = plane.a * inner + plane.b
    rows, cols = x0_ref.shape
    row_lines = (right.shape[0] // CORES, CORES)
    height = rows // CHUNKS

    def turned(at):
        return (at % outer) * inner + at // outer

    def chunk_gather(number, is_turned):
        share = pl.ds(number * height, height)
        own_sems = sems[3 + 3 * number : 6 + 3 * number]
        if is_turned:
            return LineGather(
                lambda at: left.at[turned(at), share],
                inner,
                outer,
                plane.b * outer + plane.a,
                lambda at: (row, turned(at)),
                own_sems,
            )
        return LineGather(lambda at: left.at[at, share], outer, inner, col, lambda at: (row, at), own_sems)

    def again_gather(number):
        share = pl.ds(number * height, height)
        own_sems = sems[3 * (1 + CHUNKS + number) : 3 * (2 + CHUNKS + number)]
        return LineGather(lambda at: second.at[at, share], *row_lines, row, lambda at: (at, col), own_sems)

    across_rows = LineGather(right.at.__getitem__, *row_lines, row, lambda at: (at, col), sems[0:3])
    chunks = [chunk_gather(number, is_turned) for number, is_turned in enumerate(turned_chunks(outer, inner))]
    again = [again_gather(number) for number in range(CHUNKS)]
    left[col] = x0_ref[...]
    right[row] = x0_ref[...]
    chunks[0].begin()
    across_rows.begin()
    for i in range(rows // EDGE):
        for j in range(0, cols // EDGE, 2):
            mask[i * EDGE : (i + 1) * EDGE, j * EDGE : (j + 2) * EDGE] = block_masks(mask_ref, i, j)
    acc[...] = jnp.zeros_like(acc)
    going, waiting = [across_rows, chunks[0]], chunks[1:]
    while going:
        if waiting:
            waiting[0].begin()
        begun = waiting[:1]
        waiting = waiting[1:]
        for gather in list(going):
            if next(gather.going, "end") is None:
                continue
            going.remove(gather)
            if gather in chunks:
                number = chunks.index(gather)
                share = slice(number * height, (number + 1) * height)
                for place in range(right.shape[0]):
                    add_product(acc, left, right, place, share)
                second[row, share, :] = (mask[share, :] * acc[share, :]).astype(jnp.bfloat16)
                again[number].begin()
                begun.append(again[number])
        going += begun
    acc[...] = jnp.zeros_like(acc)
    for place in range(right.shape[0]):
        add_product(acc, left, second, place)
    x3_ref[...] = mask[...] * acc[...]
    for gather in (across_rows, *chunks, *again):
        gather.drain()


def finish_kernel(scale, core_ref, ham_ref, x0_ref, x3_ref, ks_ref, sign_ref):
    ks_ref[...] = core_ref[...] + ham_ref[...]
    sign_ref[...] = (1.5 * x0_ref[...].astype(jnp.float32) - 0.5 * x3_ref[...]) / scale


def finish(scale, core_ham, ham_tile, x0, x3):
    rows, cols = core_ham.shape
    share = pl.BlockSpec((rows // 2, cols), lambda i: (i, 0))
    return pl.pallas_call(
        functools.partial(finish_kernel, scale),
        out_shape=(jax.ShapeDtypeStruct(core_ham.shape, jnp.float32),) * 2,
        grid=(2,),
        in_specs=[share] * 4,
        out_specs=(share,) * 2,
        compiler_params=pltpu.CompilerParams(vmem_limit_bytes=VMEM_LIMIT),
        name="finish",
    )(core_ham, ham_tile, x0, x3)


def body(density, core_ham, block_mask, send_blocks, task_atoms, basis, v_loc):
    row_count, col_count = lax.axis_size("row"), lax.axis_size("col")
    block_rows = density.shape[0] // EDGE
    outer = math.gcd(col_count, 4)
    inner = col_count // outer
    received, kept = send_blocks_out((outer, inner), send_blocks[0].T, density)
    k_slot = grid_step(task_atoms[:, 0].transpose(0, 2, 1), received, basis[0], v_loc)
    scale = 1.0 / math.sqrt(16.0 * block_rows * row_count)
    parts = send_blocks_back(scale, (outer, inner), kept, k_slot, block_mask.T, core_ham)
    return finish(scale, core_ham, *parts)


def solution(mesh):
    placed = (
        P("row", "col"),
        P("row", "col"),
        P("row", "col"),
        P(("row", "col"), None, None),
        P(None, ("row", "col"), None, None),
        P(("row", "col"), None, None),
        P(("row", "col"), None),
    )
    return jax.shard_map(
        body,
        mesh=mesh,
        in_specs=placed,
        out_specs=(P("row", "col"), P("row", "col")),
        check_vma=False,
    )
```

```python
import functools
import math

import jax
import jax.numpy as jnp
from jax import lax
from jax.experimental import pallas as pl
from jax.experimental.pallas import tpu as pltpu
from jax.sharding import PartitionSpec as P

ATOMS = 16
EDGE = 64
HALF = EDGE // 2
LANES = 2 * EDGE
CORES = 2
CHUNKS = 4
MESH = pl.DeviceIdType.MESH
VMEM_LIMIT = 56 * 1024 * 1024


def low_lanes():
    return lax.broadcasted_iota(jnp.int32, (HALF, LANES), 1) < EDGE


def join_pair(first, second):
    low = low_lanes()
    top = jnp.where(low, first, pltpu.roll(second, EDGE, 1))
    bottom = jnp.where(low, pltpu.roll(first, EDGE, 1), second)
    return top, bottom


def split_pair(top, bottom):
    return join_pair(top, bottom)


class Plane:
    def __init__(self, outer, inner, row_count):
        self.outer, self.inner, self.count = outer, inner, row_count * inner
        self.row, col = lax.axis_index("row"), lax.axis_index("col")
        self.a, self.b = col // inner, col % inner
        self.place = self.row * inner + self.b

    def peer(self, offset):
        return lax.rem(self.place + 1 + offset, self.count)

    def device(self, place):
        return (place // self.inner, self.a * self.inner + place % self.inner)

    def owner(self, place, outer_at):
        return (place // self.inner) * (self.outer * self.inner) + outer_at * self.inner + place % self.inner

    def on_line(self, outer_at):
        return (self.row, outer_at * self.inner + self.b)

    def greet(self, line):
        barrier = pltpu.get_barrier_semaphore()

        def signal(offset, carry):
            pl.semaphore_signal(barrier, inc=1, device_id=self.device(self.peer(offset)), device_id_type=MESH)
            return carry

        lax.fori_loop(0, self.count - 1, signal, 0)
        greet([line], self.count - 1)


def send_kernel(
    outer, inner, row_count, index_ref, lists_ref, density_ref, out_ref, kept_ref,
    own, lists, lists_smem, stage, list_sem, recv_sem, send_sem, tile_send, tile_recv, *rest
):
    plane = Plane(outer, inner, row_count)
    a = plane.a
    rows, cols = density_ref.shape
    across = cols // EDGE
    count = (rows // EDGE) * across
    slots = stage.shape[2]
    entries = LineGather(lists.at.__getitem__, outer, 1, a, plane.on_line, rest[0:3])
    arrived = (rest[3 : 2 + outer], rest[2 + outer :])
    for tile in (own, *arrived[0], *arrived[1]):
        tile[count] = jnp.zeros((HALF, LANES), tile.dtype)
    lists[a] = jnp.zeros(lists.shape[1:], jnp.int32)
    lists[a, 0 : lists_ref.shape[0], 0 : lists_ref.shape[1]] = lists_ref[...]
    for i in range(rows // EDGE):
        for j in range(0, across, 2):
            lanes = slice(j * EDGE, (j + 2) * EDGE)
            top = density_ref[i * EDGE : i * EDGE + HALF, lanes].astype(jnp.float32)
            bottom = density_ref[i * EDGE + HALF : (i + 1) * EDGE, lanes].astype(jnp.float32)
            first, second = split_pair(top, bottom)
            own[i * across + j] = first.astype(own.dtype)
            own[i * across + j + 1] = second.astype(own.dtype)
    plane.greet(entries)

    def passes(d, step):
        source, target = a - d * step, a + step
        return jnp.logical_and(
            jnp.logical_and(source >= 0, source < outer), jnp.logical_and(target >= 0, target < outer)
        )

    def pass_on(d, way, step):
        tile = arrived[way][d - 1] if d else own
        return pltpu.make_async_remote_copy(
            src_ref=tile.at[pl.ds(0, count)],
            dst_ref=arrived[way][d].at[pl.ds(0, count)],
            send_sem=tile_send.at[way, d],
            recv_sem=tile_recv.at[way, d],
            device_id=plane.on_line(a + step),
            device_id_type=MESH,
        )

    def serve(tile, source, number):
        def pick(offset, place):
            target = plane.owner(place, a)
            for slot in range(slots):
                found = number(slot, target)
                local = jnp.where(found >= 0, found, count)
                stage[source, offset, slot] = tile[local]
                kept_ref[source, place * slots + slot] = local

        def one(offset, carry):
            place = plane.peer(offset)
            pick(offset, place)
            pltpu.make_async_remote_copy(
                src_ref=stage.at[source, offset],
                dst_ref=out_ref.at[plane.owner(plane.place, source)],
                send_sem=send_sem,
                recv_sem=recv_sem,
                device_id=plane.device(place),
                device_id_type=MESH,
            ).start()
            return carry

        lax.fori_loop(0, plane.count - 1, one, 0)
        pick(plane.count - 1, plane.place)
        pltpu.make_async_copy(
            stage.at[source, plane.count - 1], out_ref.at[plane.owner(plane.place, source)], recv_sem
        ).start()

    entry_steps = entries.steps()
    for d in range(outer):
        next(entry_steps, None)
        if d:
            for way, step in enumerate((1, -1)):
                source = a - d * step

                @pl.when(jnp.logical_and(source >= 0, source < outer))
                def _():
                    copy = pltpu.make_async_copy(lists.at[source], lists_smem.at[source], list_sem)
                    copy.start()
                    copy.wait()
                    tile = arrived[way][d - 1].at[pl.ds(0, count)]
                    pltpu.make_async_copy(tile, tile, tile_recv.at[way, d - 1]).wait()

        if d < outer - 1:
            for way, step in enumerate((1, -1)):

                @pl.when(passes(d, step))
                def _():
                    pass_on(d, way, step).start()

        if d == 0:
            serve(own, a, lambda slot, at: index_ref[slot, at])
            continue
        for way, step in enumerate((1, -1)):
            source = a - d * step

            @pl.when(jnp.logical_and(source >= 0, source < outer))
            def _():
                serve(arrived[way][d - 1], source, lambda slot, at: lists_smem[source, slot, at])

    for d in range(outer - 1):
        for way, step in enumerate((1, -1)):

            @pl.when(passes(d, step))
            def _():
                pass_on(d, way, step).wait_send()

    entries.drain()
    sent = stage.at[:, pl.ds(0, plane.count - 1)]
    pltpu.make_async_copy(sent, sent, send_sem).wait()
    pltpu.make_async_copy(out_ref, out_ref, recv_sem).wait()


def up_to(size, step):
    return size + -size % step


def send_blocks_out(lines, lists, density):
    outer, inner = lines
    slots, devices = lists.shape
    row_count, col_count = lax.axis_size("row"), lax.axis_size("col")
    plane_count = row_count * inner
    count = (density.shape[0] // EDGE) * (density.shape[1] // EDGE)
    vmem = pl.BlockSpec(memory_space=pltpu.VMEM)
    return pl.pallas_call(
        functools.partial(send_kernel, outer, inner, row_count),
        out_shape=(
            jax.ShapeDtypeStruct((row_count * col_count, slots, HALF, LANES), jnp.bfloat16),
            jax.ShapeDtypeStruct((up_to(outer, 8), up_to(plane_count * slots, LANES)), jnp.int32),
        ),
        in_specs=[pl.BlockSpec(memory_space=pltpu.SMEM), vmem, vmem],
        out_specs=(pl.BlockSpec(memory_space=pl.ANY), pl.BlockSpec(memory_space=pltpu.SMEM)),
        scratch_shapes=[
            pltpu.VMEM((count + 1, HALF, LANES), jnp.bfloat16),
            pltpu.VMEM((outer, up_to(slots, 8), up_to(devices, LANES)), jnp.int32),
            pltpu.SMEM((outer, up_to(slots, 8), up_to(devices, LANES)), jnp.int32),
            pltpu.VMEM((outer, plane_count, slots, HALF, LANES), jnp.bfloat16),
            pltpu.SemaphoreType.DMA,
            pltpu.SemaphoreType.DMA,
            pltpu.SemaphoreType.DMA,
            pltpu.SemaphoreType.DMA((2, outer)),
            pltpu.SemaphoreType.DMA((2, outer)),
            *LineGather.semaphores(outer, 1),
            *[pltpu.VMEM((count + 1, HALF, LANES), jnp.bfloat16)] * (2 * (outer - 1)),
        ],
        compiler_params=pltpu.CompilerParams(
            vmem_limit_bytes=VMEM_LIMIT, collective_id=1, has_side_effects=True
        ),
        name="send_out",
    )(lists, lists, density)


def back_kernel(
    scale, outer, inner, row_count, kept_ref, mask_ref, slots_ref, core_ref, ham_ref, x0_ref, x3_ref,
    landed, wide, first_total, second_total, sums, arriving, land_sem, send_sem, line_send, line_recv, *rest
):
    plane = Plane(outer, inner, row_count)
    a, b = plane.a, plane.b
    rows, cols = core_ref.shape
    across = cols // EDGE
    count = sums.shape[1]
    slots = slots_ref.shape[1]
    terms = plane.count * slots
    line = LineGather(None, outer, 1, a, plane.on_line, (None,) * 3)
    plane.greet(line)

    def send_plane(target):
        def one(offset, carry):
            place = plane.peer(offset)
            pltpu.make_async_remote_copy(
                src_ref=slots_ref.at[plane.owner(place, target)],
                dst_ref=landed.at[target, plane.place],
                send_sem=send_sem.at[target],
                recv_sem=land_sem.at[target],
                device_id=plane.device(place),
                device_id_type=MESH,
            ).start()
            return carry

        lax.fori_loop(0, plane.count - 1, one, 0)
        pltpu.make_async_copy(
            slots_ref.at[plane.owner(plane.place, target)], landed.at[target, plane.place], land_sem.at[target]
        ).start()

    def combine(target, total):
        pltpu.make_async_copy(landed.at[target], landed.at[target], land_sem.at[target]).wait()
        wide[...] = landed[target].astype(jnp.float32).reshape(wide.shape)
        numbers = lax.broadcasted_iota(jnp.int32, (count, terms), 0)
        chosen = jnp.where(numbers == kept_ref[pl.ds(target, 1), 0:terms], 1.0, 0.0).astype(jnp.bfloat16)
        for line_at in range(HALF):
            part = wide[pl.ds(line_at, terms, stride=HALF), :].astype(jnp.bfloat16)
            total[pl.ds(line_at, count, stride=HALF), :] = jnp.dot(
                chosen, part, preferred_element_type=jnp.float32
            )

    def wait_line(target, side):
        ref = arriving.at[target, side]
        pltpu.make_async_copy(ref, ref, line_recv.at[target, side]).wait()

    def pass_on(target, step, side):
        return pltpu.make_async_remote_copy(
            src_ref=sums.at[target],
            dst_ref=arriving.at[target, side],
            send_sem=line_send.at[target],
            recv_sem=line_recv.at[target, side],
            device_id=plane.on_line(a + step),
            device_id_type=MESH,
        )

    order = [(d, step) for d in range(outer - 1, 0, -1) for step in (1, -1)] + [(0, 1)]

    def each(d, step, act):
        target = a + d * step

        @pl.when(jnp.logical_and(target >= 0, target < outer))
        def _():
            act(target)

    def nth(k, act):
        far = jnp.maximum(a, outer - 1 - a)
        near = outer - 1 - far
        up = a < outer - 1 - a
        long = far - near
        alone = jnp.where(up, a + far - k, a - far + k)
        rest = k - long
        dist = near - rest // 2
        paired = jnp.where(lax.rem(rest, 2) == 0, a + dist, a - dist)
        act(jnp.where(rest < 0, alone, paired))

    def sent_plane(target):
        sent = landed.at[target, pl.ds(0, plane.count - 1)]
        pltpu.make_async_copy(sent, sent, send_sem.at[target]).wait()

    nth(0, send_plane)
    totals = (first_total, second_total)

    def pass_total(k, with_line):
        total = totals[k % 2]

        def handle(target):
            for side, step in ((0, 1), (1, -1)):
                inside = jnp.logical_and(a - step >= 0, a - step < outer)
                fits = inside if with_line else jnp.logical_not(inside)

                @pl.when(jnp.logical_and((target - a) * step > 0, fits))
                def _():
                    if with_line:
                        wait_line(target, side)
                        total[...] += arriving[target, side].astype(jnp.float32).reshape(total.shape)
                    sums[target] = total[...].astype(jnp.bfloat16).reshape(sums.shape[1:])
                    pass_on(target, step, side).start()

        nth(k, handle)

    for k in range(outer):
        nth(k, sent_plane)
        if k + 1 < outer:
            nth(k + 1, send_plane)
        nth(k, lambda target: combine(target, totals[k % 2]))
        pass_total(k, False)
        if k:
            pass_total(k - 1, True)
    total = totals[(outer - 1) % 2]
    for side, step in ((0, 1), (1, -1)):

        @pl.when(jnp.logical_and(a - step >= 0, a - step < outer))
        def _():
            wait_line(a, side)
            total[...] += arriving[a, side].astype(jnp.float32).reshape(total.shape)

    for i in range(rows // EDGE):
        for j in range(0, across, 2):
            lanes = slice(j * EDGE, (j + 2) * EDGE)
            high, mid, low = i * EDGE, i * EDGE + HALF, (i + 1) * EDGE
            at = (i * across + j) * HALF
            top, bottom = join_pair(total[at : at + HALF, :], total[at + HALF : at + 2 * HALF, :])
            ham_ref[high:mid, lanes] = top
            ham_ref[mid:low, lanes] = bottom
            ks = core_ref[high:low, lanes] + ham_ref[high:low, lanes]
            x0_ref[high:low, lanes] = (block_masks(mask_ref, i, j) * ks * scale).astype(jnp.bfloat16)

    sign_part(plane, mask_ref, x0_ref, x3_ref, *rest)
    for d, step in order:
        if d:
            side = 0 if step > 0 else 1
            each(d, step, lambda target: pass_on(target, step, side).wait_send())


def send_blocks_back(scale, lines, kept, blocks, block_mask, core_ham):
    outer, inner = lines
    row_count, col_count = lax.axis_size("row"), lax.axis_size("col")
    row_lines = (row_count // CORES, CORES)
    plane_count = row_count * inner
    slots = blocks.shape[1]
    rows, cols = core_ham.shape
    count = (rows // EDGE) * (cols // EDGE)
    vmem = pl.BlockSpec(memory_space=pltpu.VMEM)
    return pl.pallas_call(
        functools.partial(back_kernel, scale, outer, inner, row_count),
        out_shape=(
            jax.ShapeDtypeStruct(core_ham.shape, jnp.float32),
            jax.ShapeDtypeStruct(core_ham.shape, jnp.bfloat16),
            jax.ShapeDtypeStruct(core_ham.shape, jnp.float32),
        ),
        in_specs=[vmem, vmem, pl.BlockSpec(memory_space=pl.ANY), vmem],
        out_specs=(vmem,) * 3,
        scratch_shapes=[
            pltpu.VMEM((outer, plane_count, slots, HALF, LANES), jnp.bfloat16),
            pltpu.VMEM((plane_count * slots * HALF, LANES), jnp.float32),
            pltpu.VMEM((count * HALF, LANES), jnp.float32),
            pltpu.VMEM((count * HALF, LANES), jnp.float32),
            pltpu.VMEM((outer, count, HALF, LANES), jnp.bfloat16),
            pltpu.VMEM((outer, 2, count, HALF, LANES), jnp.bfloat16),
            pltpu.SemaphoreType.DMA((outer,)),
            pltpu.SemaphoreType.DMA((outer,)),
            pltpu.SemaphoreType.DMA((outer,)),
            pltpu.SemaphoreType.DMA((outer, 2)),
            pltpu.VMEM((col_count, rows, cols), jnp.bfloat16),
            pltpu.VMEM((row_count, rows, cols), jnp.bfloat16),
            pltpu.VMEM((row_count, rows, cols), jnp.bfloat16),
            pltpu.VMEM((rows, cols), jnp.float32),
            pltpu.VMEM((rows, cols), jnp.float32),
            *LineGather.semaphores(*row_lines),
            *[
                sem
                for turned in turned_chunks(outer, inner)
                for sem in LineGather.semaphores(*((inner, outer) if turned else (outer, inner)))
            ],
            *LineGather.semaphores(*row_lines) * CHUNKS,
        ],
        compiler_params=pltpu.CompilerParams(
            vmem_limit_bytes=VMEM_LIMIT, collective_id=2, has_side_effects=True
        ),
        name="back_and_sign",
    )(kept, block_mask, blocks, core_ham)


def grid_kernel(
    chunk, atoms_ref, recv_ref, basis_hbm, vloc_ref, out_ref, sums, pair_mat, k_all, basis_ref, weighted, sem
):
    cells = basis_ref.shape[1]
    load = pltpu.make_async_copy(basis_hbm, basis_ref, sem)
    load.start()
    sums[...] = jnp.zeros_like(sums)

    owners, slots = recv_ref.shape[:2]

    def pair(owner, slot):
        return atoms_ref[0, slot, owner] * ATOMS + atoms_ref[1, slot, owner]

    def add_slots(owner, carry):
        for slot in range(slots):
            at = pair(owner, slot)
            sums[at] = sums[at] + recv_ref[owner, slot].astype(jnp.float32)
        return carry

    lax.fori_loop(0, owners, add_slots, 0)

    def assemble(a, carry):
        row = pl.multiple_of(a * EDGE, EDGE)
        for b in range(0, ATOMS, 2):
            top, bottom = join_pair(sums[a * ATOMS + b], sums[a * ATOMS + b + 1])
            lanes = slice(b * EDGE, (b + 2) * EDGE)
            pair_mat[pl.ds(row, HALF), lanes] = top.astype(jnp.bfloat16)
            pair_mat[pl.ds(row + HALF, HALF), lanes] = bottom.astype(jnp.bfloat16)
        return carry

    lax.fori_loop(0, ATOMS, assemble, 0)
    columns = 4 * EDGE
    tiles = [slice(start, start + columns) for start in range(0, ATOMS * EDGE, columns)]
    for m, high in enumerate(tiles):
        for low in tiles[m + 1 :]:
            turned = pair_mat[low, high].astype(jnp.float32).T
            pair_mat[high, low] = (pair_mat[high, low].astype(jnp.float32) + turned).astype(jnp.bfloat16)
    load.wait()

    def integrate(step, carry):
        at = pl.ds(pl.multiple_of(step * chunk, chunk), chunk)
        rho = jnp.zeros((1, chunk), jnp.float32)
        for high in tiles:
            mixed = jnp.dot(
                pair_mat[high, high.start :], basis_ref[high.start :, at], preferred_element_type=jnp.float32
            )
            rho += jnp.sum(basis_ref[high, at].astype(jnp.float32) * mixed, axis=0, keepdims=True)
        wide = basis_ref[:, at].astype(jnp.float32)
        pot = vloc_ref[:, at] + 0.5 * rho / jnp.sqrt(1.0 + rho * rho)
        weighted[:, at] = (wide * pot).astype(jnp.bfloat16)
        return carry

    lax.fori_loop(0, cells // chunk, integrate, 0)
    for n, low in enumerate(tiles):
        k_all[: low.stop, low] = lax.dot_general(
            weighted[: low.stop, :], basis_ref[low, :], (((1,), (1,)), ((), ())), preferred_element_type=jnp.float32
        )
        for high in tiles[:n]:
            k_all[low, high] = k_all[high, low].T

    def split(a, carry):
        row = pl.multiple_of(a * EDGE, EDGE)
        for b in range(0, ATOMS, 2):
            lanes = slice(b * EDGE, (b + 2) * EDGE)
            first, second = split_pair(k_all[pl.ds(row, HALF), lanes], k_all[pl.ds(row + HALF, HALF), lanes])
            sums[a * ATOMS + b] = first
            sums[a * ATOMS + b + 1] = second
        return carry

    lax.fori_loop(0, ATOMS, split, 0)

    def give_slots(owner, carry):
        for slot in range(slots):
            out_ref[owner, slot] = sums[pair(owner, slot)].astype(jnp.bfloat16)
        return carry

    lax.fori_loop(0, owners, give_slots, 0)


def grid_step(atoms, received, basis, v_loc):
    order = ATOMS * EDGE
    chunk = math.gcd(basis.shape[1], 512)
    return pl.pallas_call(
        functools.partial(grid_kernel, chunk),
        out_shape=jax.ShapeDtypeStruct(received.shape, jnp.bfloat16),
        in_specs=[
            pl.BlockSpec(memory_space=pltpu.SMEM),
            pl.BlockSpec(memory_space=pltpu.VMEM),
            pl.BlockSpec(memory_space=pl.ANY),
            pl.BlockSpec(memory_space=pltpu.VMEM),
        ],
        out_specs=pl.BlockSpec(memory_space=pltpu.VMEM),
        scratch_shapes=[
            pltpu.VMEM((ATOMS * ATOMS, HALF, LANES), jnp.float32),
            pltpu.VMEM((order, order), jnp.bfloat16),
            pltpu.VMEM((order, order), jnp.float32),
            pltpu.VMEM(basis.shape, jnp.bfloat16),
            pltpu.VMEM(basis.shape, jnp.bfloat16),
            pltpu.SemaphoreType.DMA,
        ],
        compiler_params=pltpu.CompilerParams(vmem_limit_bytes=VMEM_LIMIT),
        name="grid",
    )(atoms, received, basis, v_loc)


def block_masks(mask_ref, i, j):
    low = lax.broadcasted_iota(jnp.int32, (EDGE, LANES), 1) < EDGE
    left, right = mask_ref[j : j + 1, i : i + 1], mask_ref[j + 1 : j + 2, i : i + 1]
    return jnp.where(low, left.astype(jnp.float32), right.astype(jnp.float32))


class LineGather:
    def __init__(self, piece, outer, inner, place, device_at, sems):
        self.piece, self.outer, self.inner = piece, outer, inner
        self.a, self.b = place // inner, place % inner
        self.device_at = device_at
        self.out_sem, self.in_sem, self.recv_sem = sems
        self.sent = []

    def neighbours(self):
        a, b = self.a, self.b
        return (
            (a > 0, a - 1, b),
            (a < self.outer - 1, a + 1, b),
            (b > 0, a, b - 1),
            (b < self.inner - 1, a, b + 1),
        )

    def send(self, cond, source, target, sem):
        def describe():
            return pltpu.make_async_remote_copy(
                src_ref=self.piece(source),
                dst_ref=self.piece(source),
                send_sem=sem,
                recv_sem=self.recv_sem.at[source],
                device_id=self.device_at(target),
                device_id_type=MESH,
            )

        @pl.when(cond)
        def _():
            describe().start()

        self.sent.append((cond, describe))

    def arrive(self, source):
        pltpu.make_async_copy(self.piece(source), self.piece(source), self.recv_sem.at[source]).wait()

    def along_inner(self, cond, outer_at, inner_from, step, sem):
        target = self.b + step
        fits = jnp.logical_and(target >= 0, target < self.inner)
        self.send(
            jnp.logical_and(cond, fits), outer_at * self.inner + inner_from, self.a * self.inner + target, sem
        )

    def begin(self):
        self.going = self.steps()
        next(self.going, None)

    def steps(self):
        a, b, inner = self.a, self.b, self.inner
        for d in range(self.outer):
            for way, step in enumerate((1, -1)):
                if d == 0 and way == 1:
                    have = a >= 0
                    source = a
                else:
                    source = a - d * step
                    have = jnp.logical_and(source >= 0, source < self.outer)
                tile = source * inner + b
                if d > 0:

                    @pl.when(have)
                    def _():
                        self.arrive(tile)

                target = a + step
                fits = jnp.logical_and(target >= 0, target < self.outer)
                self.send(jnp.logical_and(have, fits), tile, target * inner + b, self.out_sem.at[d, way])
                if d > 0 or way == 0:
                    for side, hop in enumerate((1, -1)):
                        self.along_inner(have, source, b, hop, self.in_sem.at[d * 2 + way, side])
            if inner > 1 or d < self.outer - 1:
                yield
        used = 2 * self.outer
        for e in range(1, inner):
            for outer_at in range(self.outer):
                for way, step in enumerate((1, -1)):
                    origin = b - e * step
                    have = jnp.logical_and(origin >= 0, origin < inner)
                    tile = outer_at * inner + origin

                    @pl.when(have)
                    def _():
                        self.arrive(tile)

                    if e < inner - 1:
                        self.along_inner(have, outer_at, origin, step, self.in_sem.at[used, way])
                if e < inner - 1:
                    used += 1
            if e < inner - 1:
                yield

    def drain(self):
        for cond, describe in self.sent:

            @pl.when(cond)
            def _():
                describe().wait_send()

    @staticmethod
    def semaphores(outer, inner):
        return [
            pltpu.SemaphoreType.DMA((outer, 2)),
            pltpu.SemaphoreType.DMA((2 * outer + max(inner - 2, 0) * outer, 2)),
            pltpu.SemaphoreType.DMA((outer * inner,)),
        ]


def greet(gathers, others=0):
    barrier = pltpu.get_barrier_semaphore()
    count = others
    for gather in gathers:
        for cond, a, b in gather.neighbours():

            @pl.when(cond)
            def _():
                pl.semaphore_signal(
                    barrier, inc=1, device_id=gather.device_at(a * gather.inner + b), device_id_type=MESH
                )

            count = count + cond.astype(jnp.int32)
    pl.semaphore_wait(barrier, count)


def add_product(acc, left, right, place, rows=slice(None)):
    width = left.shape[2]
    share = right.shape[1] // width
    for part in range(share):
        piece = right[place, part * width : (part + 1) * width, :]
        acc[rows, :] += jnp.dot(left[place * share + part, rows, :], piece, preferred_element_type=jnp.float32)


def turned_chunks(outer, inner):
    if inner == 1 or outer == 1:
        return (False,) * CHUNKS
    share = ((outer - 1) * inner - (inner - 1)) / (2 * (outer - 1) * (inner - 1))
    straight = min(CHUNKS, max(0, round(share * CHUNKS)))
    return (False,) * straight + (True,) * (CHUNKS - straight)


def sign_part(plane, mask_ref, x0_ref, x3_ref, left, right, second, mask, acc, *sems):
    row, outer, inner = plane.row, plane.outer, plane.inner
    col = plane.a * inner + plane.b
    rows, cols = x0_ref.shape
    row_lines = (right.shape[0] // CORES, CORES)
    height = rows // CHUNKS

    def turned(at):
        return (at % outer) * inner + at // outer

    def chunk_gather(number, is_turned):
        share = pl.ds(number * height, height)
        own_sems = sems[3 + 3 * number : 6 + 3 * number]
        if is_turned:
            return LineGather(
                lambda at: left.at[turned(at), share],
                inner,
                outer,
                plane.b * outer + plane.a,
                lambda at: (row, turned(at)),
                own_sems,
            )
        return LineGather(lambda at: left.at[at, share], outer, inner, col, lambda at: (row, at), own_sems)

    def again_gather(number):
        share = pl.ds(number * height, height)
        own_sems = sems[3 * (1 + CHUNKS + number) : 3 * (2 + CHUNKS + number)]
        return LineGather(lambda at: second.at[at, share], *row_lines, row, lambda at: (at, col), own_sems)

    across_rows = LineGather(right.at.__getitem__, *row_lines, row, lambda at: (at, col), sems[0:3])
    chunks = [chunk_gather(number, is_turned) for number, is_turned in enumerate(turned_chunks(outer, inner))]
    again = [again_gather(number) for number in range(CHUNKS)]
    left[col] = x0_ref[...]
    right[row] = x0_ref[...]
    for gather in (across_rows, *chunks):
        gather.begin()
    for i in range(rows // EDGE):
        for j in range(0, cols // EDGE, 2):
            mask[i * EDGE : (i + 1) * EDGE, j * EDGE : (j + 2) * EDGE] = block_masks(mask_ref, i, j)
    acc[...] = jnp.zeros_like(acc)
    going = [across_rows, *chunks]
    while going:
        begun = []
        for gather in list(going):
            if next(gather.going, "end") is None:
                continue
            going.remove(gather)
            if gather in chunks:
                number = chunks.index(gather)
                share = slice(number * height, (number + 1) * height)
                for place in range(right.shape[0]):
                    add_product(acc, left, right, place, share)
                second[row, share, :] = (mask[share, :] * acc[share, :]).astype(jnp.bfloat16)
                again[number].begin()
                begun.append(again[number])
        going += begun
    acc[...] = jnp.zeros_like(acc)
    for place in range(right.shape[0]):
        add_product(acc, left, second, place)
    x3_ref[...] = mask[...] * acc[...]
    for gather in (across_rows, *chunks, *again):
        gather.drain()


def finish_kernel(scale, core_ref, ham_ref, x0_ref, x3_ref, ks_ref, sign_ref):
    ks_ref[...] = core_ref[...] + ham_ref[...]
    sign_ref[...] = (1.5 * x0_ref[...].astype(jnp.float32) - 0.5 * x3_ref[...]) / scale


def finish(scale, core_ham, ham_tile, x0, x3):
    rows, cols = core_ham.shape
    share = pl.BlockSpec((rows // 2, cols), lambda i: (i, 0))
    return pl.pallas_call(
        functools.partial(finish_kernel, scale),
        out_shape=(jax.ShapeDtypeStruct(core_ham.shape, jnp.float32),) * 2,
        grid=(2,),
        in_specs=[share] * 4,
        out_specs=(share,) * 2,
        compiler_params=pltpu.CompilerParams(vmem_limit_bytes=VMEM_LIMIT),
        name="finish",
    )(core_ham, ham_tile, x0, x3)


def body(density, core_ham, block_mask, send_blocks, task_atoms, basis, v_loc):
    row_count, col_count = lax.axis_size("row"), lax.axis_size("col")
    block_rows = density.shape[0] // EDGE
    outer = math.gcd(col_count, 4)
    inner = col_count // outer
    received, kept = send_blocks_out((outer, inner), send_blocks[0].T, density)
    k_slot = grid_step(task_atoms[:, 0].transpose(0, 2, 1), received, basis[0], v_loc)
    scale = 1.0 / math.sqrt(16.0 * block_rows * row_count)
    parts = send_blocks_back(scale, (outer, inner), kept, k_slot, block_mask.T, core_ham)
    return finish(scale, core_ham, *parts)


def solution(mesh):
    placed = (
        P("row", "col"),
        P("row", "col"),
        P("row", "col"),
        P(("row", "col"), None, None),
        P(None, ("row", "col"), None, None),
        P(("row", "col"), None, None),
        P(("row", "col"), None),
    )
    return jax.shard_map(
        body,
        mesh=mesh,
        in_specs=placed,
        out_specs=(P("row", "col"), P("row", "col")),
        check_vma=False,
    )
```
